128 devices in a mesh: dp: 8 (over z, core), cent: 16 (over y, x).
Axes of the slice: x: 4, y: 4, z: 4, core: 2. Of those that a mesh axis runs over, the one named last changes fastest.
Arguments:
- embeddings: bfloat16 [16384, 128], P(('dp', 'cent')), may hold values from -6 to 6
- centroids: bfloat16 [131072, 128], P('cent'), may hold values from -6 to 6
- col_mass: float32 [131072], P('cent'), may hold values from 0.3 to 3
- assignments: int32 [2, 16384], P(None, ('dp', 'cent')), may hold values from 0 to 131071, as said below
Outputs:
- new_centroids: bfloat16 [131072, 128], P('cent')
- assign_mass: float32 [2, 16384], P(None, ('dp', 'cent'))
- residuals: bfloat16 [16384, 128], P(('dp', 'cent'))
The draws below stay inside these ranges and needn't reach their ends.
Inputs may be any that keep to these rules, and one draw needn't show every extreme that they name: `assignments`: centroid k is owned by the device at cent index k // 8192 and dp index (k % 8192) // 1024. In each iteration, the 128 tokens of one device name centroids of exactly 64 distinct owners, 2 tokens each; in each iteration some owner gets 2 tokens from every device.
All inputs are finite; a program needn't handle non-finite values.
Results may differ from the reference program's by a relative error of at most 0.025.
Values may be sent and summed in bfloat16 or wider, within the bound.
No kernel may reach another device: no remote copies, remote signals or barrier semaphores. Data moves between devices by JAX's collectives and lax.ppermute only.
A program may use at most 64 MiB of HBM per device.

```python
import math
import jax
import jax.numpy as jnp
from jax import lax

D = 128
KC = 8192
TOK_DEV = 128
ITERS = 2
CENTROID_TOTAL = 131072
TOKENS = 16384
KO = 1024
CAP = 2
N_DP = 8
N_CENT = 16


def draw_assignments(key, part):
    key = jax.random.fold_in(key, 7)
    owner_devices = N_DP * N_CENT
    chosen_count = TOK_DEV // CAP
    outputs = []
    for step in range(ITERS):
        sub = jax.random.fold_in(key, step)
        key_hot, key_score, key_order, key_local = jax.random.split(sub, 4)
        onehot_matrix = jax.random.permutation(key_hot, owner_devices)[:3]
        score_boost = jnp.zeros((owner_devices,), jnp.int32).at[onehot_matrix].set(2 * owner_devices * owner_devices * owner_devices)
        affinity_matrix = jax.random.randint(key_score, (owner_devices, owner_devices), 0, owner_devices * owner_devices) * owner_devices
        affinity_matrix = affinity_matrix + jnp.arange(owner_devices, dtype=jnp.int32)[None, :] + score_boost[None, :]
        _, chosen = lax.top_k(affinity_matrix, chosen_count)
        owner_rows = jnp.repeat(chosen, CAP, axis=1)
        order_keys = jax.random.randint(key_order, (owner_devices, TOK_DEV), 0, 1 << 20) * TOK_DEV
        order_keys = order_keys + jnp.arange(TOK_DEV, dtype=jnp.int32)[None, :]
        order = jnp.argsort(order_keys, axis=1, stable=True)
        owner_rows = jnp.take_along_axis(owner_rows, order, axis=1)
        local = jax.random.randint(key_local, (owner_devices, TOK_DEV), 0, KO)
        picked_centroids = owner_rows % N_CENT * KC + owner_rows // N_CENT * KO + local
        outputs.append(picked_centroids.reshape(TOKENS).astype(jnp.int32))
    return jnp.stack(outputs)


def shard_levels(key, shape, cuts, least, high):
    loudness, own = 1.0, jax.random.fold_in(key, 6)
    for axis_at, parts in cuts:
        heights = jnp.exp(jax.random.uniform(jax.random.fold_in(own, axis_at), (parts,), jnp.float32, least / len(cuts), high / len(cuts)))
        loudness = loudness * jnp.repeat(heights, shape[axis_at] // parts).reshape([-1 if axis == axis_at else 1 for axis in range(len(shape))])
    return loudness


def normal_values(own_key, shape, scale, reach, shards=(), kind=jnp.bfloat16):
    array = jax.random.normal(own_key, shape, jnp.float32) * scale
    if len(shards) > 0:
        array = shard_levels(own_key, shape, shards, -0.22, 0.18) * array
    return jnp.clip(array, min=-reach, max=reach).astype(kind)


def setup_inputs(seed: int = 0) -> dict:
    key_of = jax.random.split(jax.random.key(seed), 5)
    embeddings = normal_values(key_of[0], (TOKENS, D), 1.0, 6.0, ((0, 128),))
    centroids = normal_values(key_of[1], (CENTROID_TOTAL, D), 1.0, 6.0, ((0, 16),))
    col_mass = jnp.clip(jnp.exp(math.log(3.0) - 2.3025851 * jax.random.uniform(key_of[2], (CENTROID_TOTAL,), jnp.float32) ** shard_levels(key_of[2], (CENTROID_TOTAL,), ((0, 16),), -0.2, 0.2)), 0.3, 3.0)
    assignments = draw_assignments(jax.random.fold_in(key_of[4], 71), 0)
    return {"embeddings": embeddings, "centroids": centroids, "col_mass": col_mass, "assignments": assignments}


softness_factor = 0.05
prior_weight = 1.0

def unit_rows(x):
    xf = x.astype(jnp.float32)
    return xf * lax.rsqrt(lax.optimization_barrier(jnp.sum(xf * xf, axis=1, keepdims=True)) + 1e-06)

def reference(embeddings, centroids, col_mass, assignments):
    xn = unit_rows(embeddings).astype(jnp.bfloat16)
    cents = unit_rows(centroids).astype(jnp.bfloat16)
    xf = xn.astype(jnp.float32)
    target = col_mass * (TOKENS / CENTROID_TOTAL)
    column_potential = jnp.ones((CENTROID_TOTAL,), jnp.float32)
    blocks = xn.reshape(TOKENS // 512, 512, D)
    masses = []
    for step in range(ITERS):

        def tile(blk):
            unscaled_logits = lax.dot_general(blk, cents, (((1,), (1,)), ((), ())), preferred_element_type=jnp.float32)
            return jnp.exp(unscaled_logits / softness_factor)

        def row_pass(blk):
            return lax.optimization_barrier(jnp.sum(tile(blk) * column_potential, axis=1))
        row_potential = 1.0 / lax.map(row_pass, blocks).reshape(TOKENS)

        def column_step(carry, pair):
            blk, scale = pair
            return (carry + lax.optimization_barrier(jnp.sum(tile(blk) * scale[:, None], axis=0)), None)
        col_sum, _ = lax.scan(column_step, jnp.zeros((CENTROID_TOTAL,), jnp.float32), (blocks, row_potential.reshape(TOKENS // 512, 512)))
        column_potential = target / col_sum
        picked_centroids = assignments[step]
        picked = cents[picked_centroids].astype(jnp.float32)
        affinity_value = lax.optimization_barrier(jnp.sum(xf * picked, axis=1))
        transport_weight = CENTROID_TOTAL * jnp.exp(affinity_value / softness_factor) * row_potential * column_potential[picked_centroids]
        acc = jax.ops.segment_sum(transport_weight[:, None] * xf, picked_centroids, num_segments=CENTROID_TOTAL)
        cents = unit_rows(prior_weight * cents.astype(jnp.float32) + acc).astype(jnp.bfloat16)
        masses.append(transport_weight)
    residuals = (xf - cents[assignments[ITERS - 1]].astype(jnp.float32)).astype(jnp.bfloat16)
    return (cents, jnp.stack(masses), residuals)
```

```python
import math

import jax
import jax.numpy as jnp
from jax import lax
from jax.experimental import pallas as pl
from jax.experimental.pallas import tpu as pltpu
from jax.sharding import PartitionSpec as P

F32, BF16 = jnp.float32, jnp.bfloat16
D = 128
TOK = 128
NC, ND = 16, 8
T = TOK * NC
KC = 8192
NO, KO = 8, 1024
SL = 256
SCALE = 20.0 * math.log2(math.e)
TOKENS, CENTROIDS = 16384, 131072
TC = 256
MIB = 2**20

NN = (((1,), (0,)), ((), ()))
NT = (((1,), (1,)), ((), ()))


def mm(a, b, dims=NN):
    return lax.dot_general(a, b, dims, preferred_element_type=F32)


def iota(shape, dim):
    return lax.broadcasted_iota(jnp.int32, shape, dim)


def unit(z):
    return z * lax.rsqrt(jnp.sum(z * z, axis=1, keepdims=True) + 1e-06)


def split(z):
    hi = z.astype(BF16)
    return hi, (z - hi.astype(F32)).astype(BF16)


def column(row):
    return jnp.concatenate(
        [
            jnp.broadcast_to(row[:, i : i + 128], (128, 128)).T
            for i in range(0, row.shape[1], 128)
        ],
        axis=0,
    )


def call(body, outs, name, flops, limit, scratch=()):
    return pl.pallas_call(
        body,
        out_shape=outs,
        scratch_shapes=list(scratch),
        name=name,
        compiler_params=pltpu.CompilerParams(vmem_limit_bytes=limit * MIB),
        cost_estimate=pl.CostEstimate(
            flops=flops, bytes_accessed=2 * MIB, transcendentals=0
        ),
    )


def shape(*dims, dtype=F32):
    return jax.ShapeDtypeStruct(dims, dtype)


def pack_kernel(emb, asg, out):
    xn = unit(emb[...].astype(F32)).astype(BF16)
    rows = []
    for it in range(2):
        a = asg[it : it + 1, :]
        owner = a >> 10
        own_f = owner.astype(F32)
        same = jnp.broadcast_to(own_f, (TOK, TOK)).T == own_f
        before = iota((TOK, TOK), 0) < iota((TOK, TOK), 1)
        rank = jnp.sum(jnp.where(same & before, 1.0, 0.0), axis=0, keepdims=True)
        code = (a & (KO - 1)) + 1
        rows.append((a >> 13, code >> 5, code & 31, (owner & 7) * 2 + rank.astype(jnp.int32)))
    zero = jnp.zeros((5, TOK), jnp.int32)
    for c in range(NC):
        out[c, 0:TOK, :] = xn
        parts = []
        for shard, hi, lo, place in rows:
            mine = shard == c
            parts += [jnp.where(mine, hi, 0), jnp.where(mine, lo, 0), place, zero]
        out[c, TOK : TOK + 16, :] = jnp.concatenate(parts, axis=0).astype(F32).astype(BF16)


def unpack_kernel(asg, rec, mass_out, res_out):
    masses = []
    for it in range(2):
        a = asg[it : it + 1, :]
        owner = a >> 10
        own_f = owner.astype(F32)
        same = jnp.broadcast_to(own_f, (TOK, TOK)).T == own_f
        before = iota((TOK, TOK), 0) < iota((TOK, TOK), 1)
        rank = jnp.sum(jnp.where(same & before, 1.0, 0.0), axis=0, keepdims=True)
        place = (owner.astype(F32) * 2.0 + rank) * 1.0
        shard = a >> 13
        row = shard.astype(F32) * 16.0 + (owner & 7).astype(F32) * 2.0 + rank
        col = column(row)
        lane = iota((TOK, 128), 1).astype(F32)
        oh = jnp.concatenate(
            [jnp.where(col == lane + 128.0 * j, 1.0, 0.0) for j in range(2)], axis=1
        ).astype(BF16)
        mrows = jnp.concatenate([rec[s, 16:32, :] for s in range(NC)], axis=0)
        m = mm(oh, mrows)
        masses.append(m.T[it : it + 1, :])
        if it == 1:
            rrows = jnp.concatenate([rec[s, 0:16, :] for s in range(NC)], axis=0)
            res_out[...] = mm(oh, rrows).astype(BF16)
    mass_out[...] = jnp.concatenate(masses, axis=0)


def cent_kernel(cent, out):
    @pl.loop(0, KC // 256)
    def _(i):
        at = pl.ds(pl.multiple_of(i * 256, 256), 256)
        out[at, :] = unit(cent[at, :].astype(F32)).astype(BF16)


def score_block(x, cblk, g, acc, weight, first):
    @pl.loop(0, T // TC)
    def _(j):
        at = pl.ds(pl.multiple_of(j * TC, TC), TC)
        s = mm(x[at, :], cblk[...], NT)
        e = jnp.exp2(s * SCALE)
        g[at, :] = e.astype(BF16)
        if weight is not None:
            e = e * weight
        part = e[:, 0:128]
        for q in range(1, KO // 128):
            part = part + e[:, q * 128 : (q + 1) * 128]
        if first:
            acc[at, :] = part
        else:
            acc[at, :] += part


def finish_rows(acc, out):
    for s in range(NC):
        r = jnp.sum(acc[s * 128 : (s + 1) * 128, :].T, axis=0, keepdims=True)
        for c in range(NC):
            out[c, s : s + 1, :] = r


def first_kernel(rec, cents, *refs):
    gs, row_out, x, acc = refs[:NO], refs[NO], refs[NO + 1], refs[NO + 2]
    for s in range(NC):
        x[s * TOK : (s + 1) * TOK, :] = rec[s, 0:TOK, :]
    for o in range(NO):
        score_block(x, cents.at[o * KO : (o + 1) * KO], gs[o], acc, None, o == 0)
    finish_rows(acc, row_out)


def owner_onehot(idcol, o):
    ids = idcol[o * 32 : (o + 1) * 32, :]
    lane = iota((32, 128), 1).astype(F32)
    return jnp.concatenate(
        [jnp.where(ids == lane + (128.0 * j + 1.0), 1.0, 0.0) for j in range(KO // 128)],
        axis=1,
    ).astype(BF16)


def slot_kernel(rec, cents, p_out, xs_out, id_out, code_out, col_out, cs_out):
    me = lax.axis_index("dp")
    for it in range(2):
        base = TOK + 8 * it
        hi = jnp.concatenate([rec[s, base : base + 1, :] for s in range(NC)], axis=1)
        lo = jnp.concatenate([rec[s, base + 1 : base + 2, :] for s in range(NC)], axis=1)
        pl_ = jnp.concatenate([rec[s, base + 2 : base + 3, :] for s in range(NC)], axis=1)
        hi = hi.astype(F32).astype(jnp.int32)
        lo = lo.astype(F32).astype(jnp.int32)
        pl_ = pl_.astype(F32).astype(jnp.int32)
        src = iota((1, T), 1) >> 7
        valid = (hi + lo) > 0
        lane32 = src * 2 + (pl_ & 1)
        owner = pl_ >> 1
        slot = jnp.where(valid, owner * 32 + lane32, -1)
        p = jnp.where(iota((SL, T), 0) == slot, 1.0, 0.0).astype(BF16)
        p_out[it] = p
        x = jnp.concatenate([rec[s, 0:TOK, :] for s in range(NC)], axis=0)
        xs_out[it] = mm(p, x).astype(BF16)
        ohl = jnp.where(iota((SL, T), 0) == jnp.where(valid, me * 32 + lane32, -1), 1.0, 0.0).astype(BF16)
        own8 = iota((8, T), 0) == owner
        digits = jnp.concatenate(
            [jnp.where(own8 & valid, hi, 0), jnp.where(own8 & valid, lo, 0)], axis=0
        ).astype(F32).astype(BF16)
        ids = mm(digits, ohl, NT)
        id_out[it] = jnp.concatenate([ids[:, 0:128], ids[:, 128:256]], axis=0).astype(BF16)
        flat = jnp.concatenate(
            [hi.astype(F32), lo.astype(F32), jnp.zeros((6, T), F32)], axis=0
        ).astype(BF16)
        both = mm(flat, p, NT)
        code = both[0:1, :] * 32.0 + both[1:2, :]
        code_out[it] = jnp.broadcast_to(code, (8, SL))
        col = column(code)
        col_out[it] = col
        if it == 0:
            for o in range(NO):
                oh = owner_onehot(col, o)
                cs_out[o * 32 : (o + 1) * 32, :] = mm(
                    oh, cents[o * KO : (o + 1) * KO, :]
                ).astype(BF16)


def colsum_kernel(it, rowp, p_in, xs_in, ids_in, cs_in, *refs):
    gs, out, w_out, ucol = refs[:NO], refs[NO], refs[NO + 1], refs[NO + 2]
    u = 1.0 / jnp.sum(rowp[...], axis=0)
    for s in range(NC):
        ucol[s * 128 : (s + 1) * 128, :] = jnp.broadcast_to(u[s : s + 1, :], (128, 128)).T.astype(BF16)
    W = 512
    for o in range(NO):
        for h in range(KO // W):

            def body(j, acc):
                at = pl.ds(pl.multiple_of(j * 128, 128), 128)
                uu = ucol[at, :]
                prod = gs[o][at, h * W : (h + 1) * W] * jnp.concatenate([uu] * (W // 128), axis=1)
                prod = prod[0:64] + prod[64:128]
                prod = (prod[0:32] + prod[32:64]).astype(F32)
                return acc + ((prod[0:8] + prod[8:16]) + (prod[16:24] + prod[24:32]))

            acc = lax.fori_loop(0, T // 128, body, jnp.zeros((8, W), F32))
            tot = jnp.sum(acc, axis=0, keepdims=True)
            row = (o * KO + h * W) // 128
            rows = jnp.concatenate(
                [tot[:, q * 128 : (q + 1) * 128] for q in range(W // 128)], axis=0
            ).astype(BF16)
            for d in range(ND):
                out[d, row : row + W // 128, :] = rows
    uflat = jnp.concatenate([u[s : s + 1, :] for s in range(NC)], axis=1)
    uhi, ulo = split(uflat)
    us = mm(jnp.concatenate([uhi, ulo, jnp.zeros((6, T), BF16)], axis=0), p_in[it], NT)
    us = column(us[0:1, :] + us[1:2, :])
    xs = xs_in[it].astype(F32)
    aff = jnp.sum(xs * cs_in[...].astype(F32), axis=1, keepdims=True)
    w = (CENTROIDS * jnp.exp2(aff * SCALE)) * us
    w_out[...] = w
    rows = (w * xs).astype(BF16)
    for d in range(ND):
        out[d, 64:320, :] = rows
        out[d, 320:352, :] = ids_in[it]


def potentials(rec, target, vbuf):
    tot = rec[0, 0:64, :].astype(F32)
    for d in range(1, ND):
        tot = tot + rec[d, 0:64, :].astype(F32)
    v = target[...] * (TOKENS / CENTROIDS) / tot
    vbuf[...] = v
    ids = rec[0, 320:352, :].astype(F32)
    for d in range(1, ND):
        ids = ids + rec[d, 320:352, :].astype(F32)
    hi = jnp.concatenate([ids[0:8], ids[16:24]], axis=1)
    lo = jnp.concatenate([ids[8:16], ids[24:32]], axis=1)
    return hi * 32.0 + lo


def own_masses(vbuf, code_in, it, w):
    code = code_in[it][0:1, :]
    lid = (code - 1.0).astype(jnp.int32)
    lid = jnp.where(code > 0.0, lid, 0)
    owner = iota((1, SL), 1) >> 5
    row = owner * 8 + (lid >> 7)
    oh = jnp.where(iota((128, SL), 0) == (lid & 127), 1.0, 0.0).astype(BF16)
    vhi, vlo = split(vbuf[...])
    got = mm(vhi, oh) + mm(vlo, oh)
    got = jnp.sum(jnp.where(iota((64, SL), 0) == row, got, 0.0), axis=0, keepdims=True)
    return w * column(got)


def refine(o, rec, codes, vbuf, old, new):
    lid = codes[o : o + 1, :] - 1.0
    pos = lid.astype(jnp.int32)
    vhi, vlo = split(vbuf[o * 8 : (o + 1) * 8, :])
    oh = jnp.where(iota((128, 256), 0) == (pos & 127), 1.0, 0.0).astype(BF16)
    got = mm(vhi, oh) + mm(vlo, oh)
    vs = jnp.sum(jnp.where(iota((8, 256), 0) == (pos >> 7), got, 0.0), axis=0, keepdims=True)
    rows = jnp.concatenate([rec[d, 64 + o * 32 : 96 + o * 32, :] for d in range(ND)], axis=0)
    for q in range(KO // 256):
        oht = jnp.where(iota((256, 256), 0) + q * 256 == pos, vs, 0.0).astype(BF16)
        at = slice(o * KO + q * 256, o * KO + (q + 1) * 256)
        z = old[at, :].astype(F32) + mm(oht, rows)
        new[at, :] = unit(z).astype(BF16)


def second_kernel(rec, target, code_in, col_in, w_in, old, pay, *refs):
    new, gs, row_out, mass_out, cs_out = refs[0], refs[1 : 1 + NO], refs[1 + NO], refs[2 + NO], refs[3 + NO]
    x, acc, vbuf = refs[4 + NO :]
    for s in range(NC):
        x[s * TOK : (s + 1) * TOK, :] = pay[s, 0:TOK, :]
    codes = potentials(rec, target, vbuf)
    mass_out[...] = own_masses(vbuf, code_in, 0, w_in[...])
    col = col_in[1]
    for o in range(NO):
        refine(o, rec, codes, vbuf, old, new)
        cblk = new.at[o * KO : (o + 1) * KO]
        cs_out[o * 32 : (o + 1) * 32, :] = mm(owner_onehot(col, o), cblk[...]).astype(BF16)
        vrow = jnp.concatenate([vbuf[o * 8 + q : o * 8 + q + 1, :] for q in range(8)], axis=1)
        score_block(x, cblk, gs[o], acc, vrow, o == 0)
    finish_rows(acc, row_out)


def last_kernel(rec, target, code_in, col_in, xs_in, w_in, mass1, old, new, out, vbuf):
    codes = potentials(rec, target, vbuf)
    mass2 = own_masses(vbuf, code_in, 1, w_in[...])
    lane = iota((SL, 128), 1)
    m = jnp.where(lane == 0, mass1[...], jnp.where(lane == 1, mass2, 0.0))
    col = col_in[1]
    res = []
    for o in range(NO):
        refine(o, rec, codes, vbuf, old, new)
        res.append(mm(owner_onehot(col, o), new[o * KO : (o + 1) * KO, :]))
    r = xs_in[1].astype(F32) - jnp.concatenate(res, axis=0)
    i, j = iota((SL, SL), 0), iota((SL, SL), 1)
    want = ((i >> 1) & 7) * 32 + (i >> 4) * 2 + (i & 1)
    perm = jnp.where(j == want, 1.0, 0.0).astype(BF16)
    r = mm(perm, r.astype(BF16)).astype(BF16)
    m = mm(perm, m.astype(BF16)).astype(BF16)
    for s in range(NC):
        out[s, 0:16, :] = r[s * 16 : (s + 1) * 16]
        out[s, 16:32, :] = m[s * 16 : (s + 1) * 16]


def exchange(x, axis):
    return lax.all_to_all(x, axis, 0, 0, tiled=True)


def on_device(embeddings, centroids, col_mass, assignments):
    target = col_mass.reshape(KC // 128, 128)
    gshape = tuple(pltpu.VMEM((T, KO), BF16) for _ in range(NO))
    sums = shape(NC, NC, 128)
    xacc = (pltpu.VMEM((T, D), BF16), pltpu.VMEM((T, 128), F32))
    vbuf = (pltpu.VMEM((KC // 128, 128), F32),)
    pay = call(pack_kernel, shape(NC, TOK + 16, 128, dtype=BF16), "pack", 10**6, 8)(
        embeddings, assignments
    )
    rec = exchange(pay, "cent")
    c0 = call(cent_kernel, shape(KC, D, dtype=BF16), "cents", 10**9, 12)(centroids)
    *g, rows = call(first_kernel, gshape + (sums,), "first", 10**10, 12, xacc)(rec, c0)
    rows = exchange(rows, "cent")
    p, xs, ids, code, col, cs = call(
        slot_kernel,
        (
            shape(2, SL, T, dtype=BF16),
            shape(2, SL, D, dtype=BF16),
            shape(2, 32, 128, dtype=BF16),
            shape(2, 8, SL),
            shape(2, SL, 128),
            shape(SL, D, dtype=BF16),
        ),
        "slots",
        10**9,
        16,
    )(rec, c0)

    def columns(it, rows, cs, g):
        def body(*refs):
            colsum_kernel(it, *refs)

        out, w = call(
            body,
            (shape(ND, 352, 128, dtype=BF16), shape(SL, 128)),
            f"columns{it}",
            10**9,
            12,
            (pltpu.VMEM((T, 128), BF16),),
        )(rows, p, xs, ids, cs, *g)
        return exchange(out, "dp"), w

    got, w = columns(0, rows, cs, g)
    c1, *rest = call(
        second_kernel,
        (shape(KC, D, dtype=BF16),) + gshape + (sums, shape(SL, 128), shape(SL, D, dtype=BF16)),
        "second",
        10**10,
        14,
        xacc + vbuf,
    )(got, target, code, col, w, c0, rec)
    g, (rows, mass1, cs) = rest[:NO], rest[NO:]
    rows = exchange(rows, "cent")
    got, w = columns(1, rows, cs, g)
    c2, out = call(
        last_kernel,
        (shape(KC, D, dtype=BF16), shape(NC, 32, 128, dtype=BF16)),
        "last",
        10**9,
        14,
        vbuf,
    )(got, target, code, col, xs, w, mass1, c1)
    back = exchange(out, "cent")
    mass, res = call(unpack_kernel, (shape(2, TOK), shape(TOK, D, dtype=BF16)), "unpack", 10**6, 8)(
        assignments, back
    )
    return c2, mass, res


def solution(mesh):
    in_specs = (P(("dp", "cent"), None), P("cent", None), P("cent"), P(None, ("dp", "cent")))
    out_specs = (P("cent", None), P(None, ("dp", "cent")), P(("dp", "cent"), None))
    return jax.shard_map(
        on_device, mesh=mesh, in_specs=in_specs, out_specs=out_specs, check_vma=False
    )
```

```python
import math

import jax
import jax.numpy as jnp
from jax import lax
from jax.experimental import pallas as pl
from jax.experimental.pallas import tpu as pltpu
from jax.sharding import PartitionSpec as P

F32, BF16 = jnp.float32, jnp.bfloat16
D = 128
TOK = 128
NC, ND = 16, 8
T = TOK * NC
KC = 8192
NO, KO = 8, 1024
SL = 256
SCALE = 20.0 * math.log2(math.e)
TOKENS, CENTROIDS = 16384, 131072
KW = 256
MIB = 2**20

NN = (((1,), (0,)), ((), ()))
NT = (((1,), (1,)), ((), ()))


def mm(a, b, dims=NN):
    return lax.dot_general(a, b, dims, preferred_element_type=F32)


def iota(shape, dim):
    return lax.broadcasted_iota(jnp.int32, shape, dim)


def unit(z):
    return z * lax.rsqrt(jnp.sum(z * z, axis=1, keepdims=True) + 1e-06)


def split(z):
    hi = z.astype(BF16)
    return hi, (z - hi.astype(F32)).astype(BF16)


def column(row):
    return jnp.concatenate(
        [
            jnp.broadcast_to(row[:, i : i + 128], (128, 128)).T
            for i in range(0, row.shape[1], 128)
        ],
        axis=0,
    )


def call(body, outs, name, flops, limit, scratch=()):
    return pl.pallas_call(
        body,
        out_shape=outs,
        scratch_shapes=list(scratch),
        name=name,
        compiler_params=pltpu.CompilerParams(vmem_limit_bytes=limit * MIB),
        cost_estimate=pl.CostEstimate(
            flops=flops, bytes_accessed=2 * MIB, transcendentals=0
        ),
    )


def shape(*dims, dtype=F32):
    return jax.ShapeDtypeStruct(dims, dtype)


def pack_kernel(emb, asg, out):
    xn = unit(emb[...].astype(F32)).astype(BF16)
    rows = []
    for it in range(2):
        a = asg[it : it + 1, :]
        owner = a >> 10
        own_f = owner.astype(F32)
        same = jnp.broadcast_to(own_f, (TOK, TOK)).T == own_f
        before = iota((TOK, TOK), 0) < iota((TOK, TOK), 1)
        rank = jnp.sum(jnp.where(same & before, 1.0, 0.0), axis=0, keepdims=True)
        code = (a & (KO - 1)) + 1
        rows.append((a >> 13, code >> 5, code & 31, (owner & 7) * 2 + rank.astype(jnp.int32)))
    zero = jnp.zeros((5, TOK), jnp.int32)
    for c in range(NC):
        out[c, 0:TOK, :] = xn
        parts = []
        for shard, hi, lo, place in rows:
            mine = shard == c
            parts += [jnp.where(mine, hi, 0), jnp.where(mine, lo, 0), place, zero]
        out[c, TOK : TOK + 16, :] = jnp.concatenate(parts, axis=0).astype(F32).astype(BF16)


def unpack_kernel(asg, rec, mass_out, res_out):
    masses = []
    for it in range(2):
        a = asg[it : it + 1, :]
        owner = a >> 10
        own_f = owner.astype(F32)
        same = jnp.broadcast_to(own_f, (TOK, TOK)).T == own_f
        before = iota((TOK, TOK), 0) < iota((TOK, TOK), 1)
        rank = jnp.sum(jnp.where(same & before, 1.0, 0.0), axis=0, keepdims=True)
        place = (owner.astype(F32) * 2.0 + rank) * 1.0
        shard = a >> 13
        row = shard.astype(F32) * 16.0 + (owner & 7).astype(F32) * 2.0 + rank
        col = column(row)
        lane = iota((TOK, 128), 1).astype(F32)
        oh = jnp.concatenate(
            [jnp.where(col == lane + 128.0 * j, 1.0, 0.0) for j in range(2)], axis=1
        ).astype(BF16)
        mrows = jnp.concatenate([rec[s, 16:32, :] for s in range(NC)], axis=0)
        m = mm(oh, mrows)
        masses.append(m.T[it : it + 1, :])
        if it == 1:
            rrows = jnp.concatenate([rec[s, 0:16, :] for s in range(NC)], axis=0)
            res_out[...] = mm(oh, rrows).astype(BF16)
    mass_out[...] = jnp.concatenate(masses, axis=0)


def cent_kernel(cent, out):
    @pl.loop(0, KC // 256)
    def _(i):
        at = pl.ds(pl.multiple_of(i * 256, 256), 256)
        out[at, :] = unit(cent[at, :].astype(F32)).astype(BF16)


def score_block(x, cblk, g, acc, weight, first):
    part = None
    for k in range(0, KO, KW):
        e = jnp.exp2(mm(x[...], cblk[k : k + KW, :], NT) * SCALE)
        g[:, k : k + KW] = e.astype(BF16)
        for q in range(0, KW, 128):
            t = e[:, q : q + 128]
            if weight is not None:
                t = t * weight[:, k + q : k + q + 128]
            part = t if part is None else part + t
    if first:
        acc[...] = part
    else:
        acc[...] += part


def finish_rows(acc, out):
    for s in range(NC):
        r = jnp.sum(acc[s * 128 : (s + 1) * 128, :].T, axis=0, keepdims=True)
        for c in range(NC):
            out[c, s : s + 1, :] = r


def first_kernel(rec, cents, *refs):
    gs, row_out, x, acc = refs[:NO], refs[NO], refs[NO + 1], refs[NO + 2]
    for s in range(NC):
        x[s * TOK : (s + 1) * TOK, :] = rec[s, 0:TOK, :]
    for o in range(NO):
        score_block(x, cents.at[o * KO : (o + 1) * KO], gs[o], acc, None, o == 0)
    finish_rows(acc, row_out)


def owner_onehot(idcol, o):
    ids = idcol[o * 32 : (o + 1) * 32, :]
    lane = iota((32, 128), 1).astype(F32)
    return jnp.concatenate(
        [jnp.where(ids == lane + (128.0 * j + 1.0), 1.0, 0.0) for j in range(KO // 128)],
        axis=1,
    ).astype(BF16)


def slot_kernel(rec, cents, p_out, xs_out, id_out, code_out, col_out, cs_out):
    me = lax.axis_index("dp")
    for it in range(2):
        base = TOK + 8 * it
        hi = jnp.concatenate([rec[s, base : base + 1, :] for s in range(NC)], axis=1)
        lo = jnp.concatenate([rec[s, base + 1 : base + 2, :] for s in range(NC)], axis=1)
        pl_ = jnp.concatenate([rec[s, base + 2 : base + 3, :] for s in range(NC)], axis=1)
        hi = hi.astype(F32).astype(jnp.int32)
        lo = lo.astype(F32).astype(jnp.int32)
        pl_ = pl_.astype(F32).astype(jnp.int32)
        src = iota((1, T), 1) >> 7
        valid = (hi + lo) > 0
        lane32 = src * 2 + (pl_ & 1)
        owner = pl_ >> 1
        slot = jnp.where(valid, owner * 32 + lane32, -1)
        p = jnp.where(iota((SL, T), 0) == slot, 1.0, 0.0).astype(BF16)
        p_out[it] = p
        x = jnp.concatenate([rec[s, 0:TOK, :] for s in range(NC)], axis=0)
        xs_out[it] = mm(p, x).astype(BF16)
        ohl = jnp.where(iota((SL, T), 0) == jnp.where(valid, me * 32 + lane32, -1), 1.0, 0.0).astype(BF16)
        own8 = iota((8, T), 0) == owner
        digits = jnp.concatenate(
            [jnp.where(own8 & valid, hi, 0), jnp.where(own8 & valid, lo, 0)], axis=0
        ).astype(F32).astype(BF16)
        ids = mm(digits, ohl, NT)
        id_out[it] = jnp.concatenate([ids[:, 0:128], ids[:, 128:256]], axis=0).astype(BF16)
        flat = jnp.concatenate(
            [hi.astype(F32), lo.astype(F32), jnp.zeros((6, T), F32)], axis=0
        ).astype(BF16)
        both = mm(flat, p, NT)
        code = both[0:1, :] * 32.0 + both[1:2, :]
        code_out[it] = jnp.broadcast_to(code, (8, SL))
        col = column(code)
        col_out[it] = col
        if it == 0:
            for o in range(NO):
                oh = owner_onehot(col, o)
                cs_out[o * 32 : (o + 1) * 32, :] = mm(
                    oh, cents[o * KO : (o + 1) * KO, :]
                ).astype(BF16)


def colsum_kernel(it, rowp, p_in, xs_in, ids_in, cs_in, *refs):
    gs, out, w_out, ucol = refs[:NO], refs[NO], refs[NO + 1], refs[NO + 2]
    u = 1.0 / jnp.sum(rowp[...], axis=0)
    for s in range(NC):
        ucol[s * 128 : (s + 1) * 128, :] = jnp.broadcast_to(u[s : s + 1, :], (128, 128)).T.astype(BF16)
    W = 512
    for o in range(NO):
        for h in range(KO // W):

            def body(j, acc):
                at = pl.ds(pl.multiple_of(j * 128, 128), 128)
                uu = ucol[at, :]
                prod = gs[o][at, h * W : (h + 1) * W] * jnp.concatenate([uu] * (W // 128), axis=1)
                prod = prod[0:64] + prod[64:128]
                prod = (prod[0:32] + prod[32:64]).astype(F32)
                return acc + ((prod[0:8] + prod[8:16]) + (prod[16:24] + prod[24:32]))

            acc = lax.fori_loop(0, T // 128, body, jnp.zeros((8, W), F32))
            tot = jnp.sum(acc, axis=0, keepdims=True)
            row = (o * KO + h * W) // 128
            rows = jnp.concatenate(
                [tot[:, q * 128 : (q + 1) * 128] for q in range(W // 128)], axis=0
            ).astype(BF16)
            for d in range(ND):
                out[d, row : row + W // 128, :] = rows
    uflat = jnp.concatenate([u[s : s + 1, :] for s in range(NC)], axis=1)
    uhi, ulo = split(uflat)
    us = mm(jnp.concatenate([uhi, ulo, jnp.zeros((6, T), BF16)], axis=0), p_in[it], NT)
    us = column(us[0:1, :] + us[1:2, :])
    xs = xs_in[it].astype(F32)
    aff = jnp.sum(xs * cs_in[...].astype(F32), axis=1, keepdims=True)
    w = (CENTROIDS * jnp.exp2(aff * SCALE)) * us
    w_out[...] = w
    rows = (w * xs).astype(BF16)
    for d in range(ND):
        out[d, 64:320, :] = rows
        out[d, 320:352, :] = ids_in[it]


def potentials(rec, target, vbuf):
    tot = rec[0, 0:64, :].astype(F32)
    for d in range(1, ND):
        tot = tot + rec[d, 0:64, :].astype(F32)
    v = target[...] * (TOKENS / CENTROIDS) / tot
    vbuf[...] = v
    ids = rec[0, 320:352, :].astype(F32)
    for d in range(1, ND):
        ids = ids + rec[d, 320:352, :].astype(F32)
    hi = jnp.concatenate([ids[0:8], ids[16:24]], axis=1)
    lo = jnp.concatenate([ids[8:16], ids[24:32]], axis=1)
    return hi * 32.0 + lo


def own_masses(vbuf, code_in, it, w):
    code = code_in[it][0:1, :]
    lid = (code - 1.0).astype(jnp.int32)
    lid = jnp.where(code > 0.0, lid, 0)
    owner = iota((1, SL), 1) >> 5
    row = owner * 8 + (lid >> 7)
    oh = jnp.where(iota((128, SL), 0) == (lid & 127), 1.0, 0.0).astype(BF16)
    vhi, vlo = split(vbuf[...])
    got = mm(vhi, oh) + mm(vlo, oh)
    got = jnp.sum(jnp.where(iota((64, SL), 0) == row, got, 0.0), axis=0, keepdims=True)
    return w * column(got)


def refine(o, rec, codes, vbuf, old, new):
    lid = codes[o : o + 1, :] - 1.0
    pos = lid.astype(jnp.int32)
    vhi, vlo = split(vbuf[o * 8 : (o + 1) * 8, :])
    oh = jnp.where(iota((128, 256), 0) == (pos & 127), 1.0, 0.0).astype(BF16)
    got = mm(vhi, oh) + mm(vlo, oh)
    vs = jnp.sum(jnp.where(iota((8, 256), 0) == (pos >> 7), got, 0.0), axis=0, keepdims=True)
    rows = jnp.concatenate([rec[d, 64 + o * 32 : 96 + o * 32, :] for d in range(ND)], axis=0)
    for q in range(KO // 256):
        oht = jnp.where(iota((256, 256), 0) + q * 256 == pos, vs, 0.0).astype(BF16)
        at = slice(o * KO + q * 256, o * KO + (q + 1) * 256)
        z = old[at, :].astype(F32) + mm(oht, rows)
        new[at, :] = unit(z).astype(BF16)


def second_kernel(rec, target, code_in, col_in, w_in, old, pay, *refs):
    new, gs, row_out, mass_out, cs_out = refs[0], refs[1 : 1 + NO], refs[1 + NO], refs[2 + NO], refs[3 + NO]
    x, acc, vbuf = refs[4 + NO :]
    for s in range(NC):
        x[s * TOK : (s + 1) * TOK, :] = pay[s, 0:TOK, :]
    codes = potentials(rec, target, vbuf)
    mass_out[...] = own_masses(vbuf, code_in, 0, w_in[...])
    col = col_in[1]
    for o in range(NO):
        refine(o, rec, codes, vbuf, old, new)
        cblk = new.at[o * KO : (o + 1) * KO]
        cs_out[o * 32 : (o + 1) * 32, :] = mm(owner_onehot(col, o), cblk[...]).astype(BF16)
        vrow = jnp.concatenate([vbuf[o * 8 + q : o * 8 + q + 1, :] for q in range(8)], axis=1)
        score_block(x, cblk, gs[o], acc, vrow, o == 0)
    finish_rows(acc, row_out)


def last_kernel(rec, target, code_in, col_in, xs_in, w_in, mass1, old, new, out, vbuf):
    codes = potentials(rec, target, vbuf)
    mass2 = own_masses(vbuf, code_in, 1, w_in[...])
    lane = iota((SL, 128), 1)
    m = jnp.where(lane == 0, mass1[...], jnp.where(lane == 1, mass2, 0.0))
    col = col_in[1]
    res = []
    for o in range(NO):
        refine(o, rec, codes, vbuf, old, new)
        res.append(mm(owner_onehot(col, o), new[o * KO : (o + 1) * KO, :]))
    r = xs_in[1].astype(F32) - jnp.concatenate(res, axis=0)
    i, j = iota((SL, SL), 0), iota((SL, SL), 1)
    want = ((i >> 1) & 7) * 32 + (i >> 4) * 2 + (i & 1)
    perm = jnp.where(j == want, 1.0, 0.0).astype(BF16)
    r = mm(perm, r.astype(BF16)).astype(BF16)
    m = mm(perm, m.astype(BF16)).astype(BF16)
    for s in range(NC):
        out[s, 0:16, :] = r[s * 16 : (s + 1) * 16]
        out[s, 16:32, :] = m[s * 16 : (s + 1) * 16]


def exchange(x, axis):
    return lax.all_to_all(x, axis, 0, 0, tiled=True)


def on_device(embeddings, centroids, col_mass, assignments):
    target = col_mass.reshape(KC // 128, 128)
    gshape = tuple(pltpu.VMEM((T, KO), BF16) for _ in range(NO))
    sums = shape(NC, NC, 128)
    xacc = (pltpu.VMEM((T, D), BF16), pltpu.VMEM((T, 128), F32))
    vbuf = (pltpu.VMEM((KC // 128, 128), F32),)
    pay = call(pack_kernel, shape(NC, TOK + 16, 128, dtype=BF16), "pack", 10**6, 8)(
        embeddings, assignments
    )
    rec = exchange(pay, "cent")
    c0 = call(cent_kernel, shape(KC, D, dtype=BF16), "cents", 10**9, 12)(centroids)
    p, xs, ids, code, col, cs = call(
        slot_kernel,
        (
            shape(2, SL, T, dtype=BF16),
            shape(2, SL, D, dtype=BF16),
            shape(2, 32, 128, dtype=BF16),
            shape(2, 8, SL),
            shape(2, SL, 128),
            shape(SL, D, dtype=BF16),
        ),
        "slots",
        10**9,
        16,
    )(rec, c0)

    rec, c0, xs = lax.optimization_barrier((rec, c0, xs))
    *g, rows = call(first_kernel, gshape + (sums,), "first", 10**10, 12, xacc)(rec, c0)
    rows = exchange(rows, "cent")
    def columns(it, rows, cs, g):
        def body(*refs):
            colsum_kernel(it, *refs)

        out, w = call(
            body,
            (shape(ND, 352, 128, dtype=BF16), shape(SL, 128)),
            f"columns{it}",
            10**9,
            12,
            (pltpu.VMEM((T, 128), BF16),),
        )(rows, p, xs, ids, cs, *g)
        return exchange(out, "dp"), w

    got, w = columns(0, rows, cs, g)
    c1, *rest = call(
        second_kernel,
        (shape(KC, D, dtype=BF16),) + gshape + (sums, shape(SL, 128), shape(SL, D, dtype=BF16)),
        "second",
        10**10,
        14,
        xacc + vbuf,
    )(got, target, code, col, w, c0, rec)
    g, (rows, mass1, cs) = rest[:NO], rest[NO:]
    rows = exchange(rows, "cent")
    got, w = columns(1, rows, cs, g)
    c2, out = call(
        last_kernel,
        (shape(KC, D, dtype=BF16), shape(NC, 32, 128, dtype=BF16)),
        "last",
        10**9,
        14,
        vbuf,
    )(got, target, code, col, xs, w, mass1, c1)
    back = exchange(out, "cent")
    mass, res = call(unpack_kernel, (shape(2, TOK), shape(TOK, D, dtype=BF16)), "unpack", 10**6, 8)(
        assignments, back
    )
    return c2, mass, res


def solution(mesh):
    in_specs = (P(("dp", "cent"), None), P("cent", None), P("cent"), P(None, ("dp", "cent")))
    out_specs = (P("cent", None), P(None, ("dp", "cent")), P(("dp", "cent"), None))
    return jax.shard_map(
        on_device, mesh=mesh, in_specs=in_specs, out_specs=out_specs, check_vma=False
    )
```

```python
import math

import jax
import jax.numpy as jnp
from jax import lax
from jax.experimental import pallas as pl
from jax.experimental.pallas import tpu as pltpu
from jax.sharding import PartitionSpec as P

F32, BF16 = jnp.float32, jnp.bfloat16
D = 128
TOK = 128
NC, ND = 16, 8
T = TOK * NC
KC = 8192
NO, KO = 8, 1024
SL = 256
SCALE = 20.0 * math.log2(math.e)
TOKENS, CENTROIDS = 16384, 131072
KW = 256
MIB = 2**20

NN = (((1,), (0,)), ((), ()))
NT = (((1,), (1,)), ((), ()))


def mm(a, b, dims=NN):
    return lax.dot_general(a, b, dims, preferred_element_type=F32)


def iota(shape, dim):
    return lax.broadcasted_iota(jnp.int32, shape, dim)


def unit(z):
    return z * lax.rsqrt(jnp.sum(z * z, axis=1, keepdims=True) + 1e-06)


def split(z):
    hi = z.astype(BF16)
    return hi, (z - hi.astype(F32)).astype(BF16)


def column(row):
    return jnp.concatenate(
        [
            jnp.broadcast_to(row[:, i : i + 128], (128, 128)).T
            for i in range(0, row.shape[1], 128)
        ],
        axis=0,
    )


def call(body, outs, name, flops, limit, scratch=()):
    return pl.pallas_call(
        body,
        out_shape=outs,
        scratch_shapes=list(scratch),
        name=name,
        compiler_params=pltpu.CompilerParams(vmem_limit_bytes=limit * MIB),
        cost_estimate=pl.CostEstimate(
            flops=flops, bytes_accessed=2 * MIB, transcendentals=0
        ),
    )


def shape(*dims, dtype=F32):
    return jax.ShapeDtypeStruct(dims, dtype)


def pack_kernel(emb, asg, out):
    xn = unit(emb[...].astype(F32)).astype(BF16)
    rows = []
    for it in range(2):
        a = asg[it : it + 1, :]
        owner = a >> 10
        own_f = owner.astype(F32)
        same = jnp.broadcast_to(own_f, (TOK, TOK)).T == own_f
        before = iota((TOK, TOK), 0) < iota((TOK, TOK), 1)
        rank = jnp.sum(jnp.where(same & before, 1.0, 0.0), axis=0, keepdims=True)
        code = (a & (KO - 1)) + 1
        rows.append((a >> 13, code >> 5, code & 31, (owner & 7) * 2 + rank.astype(jnp.int32)))
    zero = jnp.zeros((5, TOK), jnp.int32)
    for c in range(NC):
        out[c, 0:TOK, :] = xn
        parts = []
        for shard, hi, lo, place in rows:
            mine = shard == c
            parts += [jnp.where(mine, hi, 0), jnp.where(mine, lo, 0), place, zero]
        out[c, TOK : TOK + 16, :] = jnp.concatenate(parts, axis=0).astype(F32).astype(BF16)


def unpack_kernel(asg, rec, mass_out, res_out):
    masses = []
    for it in range(2):
        a = asg[it : it + 1, :]
        owner = a >> 10
        own_f = owner.astype(F32)
        same = jnp.broadcast_to(own_f, (TOK, TOK)).T == own_f
        before = iota((TOK, TOK), 0) < iota((TOK, TOK), 1)
        rank = jnp.sum(jnp.where(same & before, 1.0, 0.0), axis=0, keepdims=True)
        place = (owner.astype(F32) * 2.0 + rank) * 1.0
        shard = a >> 13
        row = shard.astype(F32) * 16.0 + (owner & 7).astype(F32) * 2.0 + rank
        col = column(row)
        lane = iota((TOK, 128), 1).astype(F32)
        oh = jnp.concatenate(
            [jnp.where(col == lane + 128.0 * j, 1.0, 0.0) for j in range(2)], axis=1
        ).astype(BF16)
        mrows = jnp.concatenate([rec[s, 16:32, :] for s in range(NC)], axis=0)
        m = mm(oh, mrows)
        masses.append(m.T[it : it + 1, :])
        if it == 1:
            rrows = jnp.concatenate([rec[s, 0:16, :] for s in range(NC)], axis=0)
            res_out[...] = mm(oh, rrows).astype(BF16)
    mass_out[...] = jnp.concatenate(masses, axis=0)


def cent_kernel(cent, out):
    @pl.loop(0, KC // 256)
    def _(i):
        at = pl.ds(pl.multiple_of(i * 256, 256), 256)
        out[at, :] = unit(cent[at, :].astype(F32)).astype(BF16)


def score_block(x, cblk, g, acc, weight, first):
    part = None
    for k in range(0, KO, KW):
        e = jnp.exp2(mm(x[...], cblk[k : k + KW, :], NT) * SCALE)
        g[:, k : k + KW] = e.astype(BF16)
        for q in range(0, KW, 128):
            t = e[:, q : q + 128]
            if weight is not None:
                t = t * weight[:, k + q : k + q + 128]
            part = t if part is None else part + t
    if first:
        acc[...] = part
    else:
        acc[...] += part


def finish_rows(acc, out):
    hi, lo = split(acc[...])
    one = jnp.ones((8, 128), BF16)
    r = mm(one, hi, NT) + mm(one, lo, NT)
    r = jnp.concatenate([r[0:1, s * 128 : (s + 1) * 128] for s in range(NC)], axis=0)
    for c in range(NC):
        out[c] = r


def first_kernel(rec, cents, *refs):
    gs, row_out, x, acc = refs[:NO], refs[NO], refs[NO + 1], refs[NO + 2]
    for s in range(NC):
        x[s * TOK : (s + 1) * TOK, :] = rec[s, 0:TOK, :]
    for o in range(NO):
        score_block(x, cents.at[o * KO : (o + 1) * KO], gs[o], acc, None, o == 0)
    finish_rows(acc, row_out)


def owner_onehot(idcol, o):
    ids = idcol[o * 32 : (o + 1) * 32, :]
    lane = iota((32, 128), 1).astype(F32)
    return jnp.concatenate(
        [jnp.where(ids == lane + (128.0 * j + 1.0), 1.0, 0.0) for j in range(KO // 128)],
        axis=1,
    ).astype(BF16)


def slot_kernel(it, rec, *refs):
    me = lax.axis_index("dp")
    if it == 0:
        cents, p_out, xs_out, id_out, code_out, col_out, cs_out = refs
    else:
        p_out, xs_out, id_out, code_out, col_out = refs
    base = TOK + 8 * it
    hi = jnp.concatenate([rec[s, base : base + 1, :] for s in range(NC)], axis=1)
    lo = jnp.concatenate([rec[s, base + 1 : base + 2, :] for s in range(NC)], axis=1)
    pl_ = jnp.concatenate([rec[s, base + 2 : base + 3, :] for s in range(NC)], axis=1)
    hi = hi.astype(F32).astype(jnp.int32)
    lo = lo.astype(F32).astype(jnp.int32)
    pl_ = pl_.astype(F32).astype(jnp.int32)
    src = iota((1, T), 1) >> 7
    valid = (hi + lo) > 0
    lane32 = src * 2 + (pl_ & 1)
    owner = pl_ >> 1
    slot = jnp.where(valid, owner * 32 + lane32, -1)
    p = jnp.where(iota((SL, T), 0) == slot, 1.0, 0.0).astype(BF16)
    p_out[...] = p
    x = jnp.concatenate([rec[s, 0:TOK, :] for s in range(NC)], axis=0)
    xs_out[...] = mm(p, x).astype(BF16)
    ohl = jnp.where(iota((SL, T), 0) == jnp.where(valid, me * 32 + lane32, -1), 1.0, 0.0).astype(BF16)
    own8 = iota((8, T), 0) == owner
    digits = jnp.concatenate(
        [jnp.where(own8 & valid, hi, 0), jnp.where(own8 & valid, lo, 0)], axis=0
    ).astype(F32).astype(BF16)
    ids = mm(digits, ohl, NT)
    id_out[...] = jnp.concatenate([ids[:, 0:128], ids[:, 128:256]], axis=0).astype(BF16)
    flat = jnp.concatenate(
        [hi.astype(F32), lo.astype(F32), jnp.zeros((6, T), F32)], axis=0
    ).astype(BF16)
    both = mm(flat, p, NT)
    code = both[0:1, :] * 32.0 + both[1:2, :]
    code_out[...] = jnp.broadcast_to(code, (8, SL))
    col = column(code)
    col_out[...] = col
    if it == 0:
        for o in range(NO):
            oh = owner_onehot(col, o)
            cs_out[o * 32 : (o + 1) * 32, :] = mm(
                oh, cents[o * KO : (o + 1) * KO, :]
            ).astype(BF16)


def colsum_kernel(rowp, p_in, xs_in, ids_in, cs_in, *refs):
    gs, out, w_out, ucol = refs[:NO], refs[NO], refs[NO + 1], refs[NO + 2]
    u = 1.0 / jnp.sum(rowp[...], axis=0)
    for s in range(NC):
        ucol[s * 128 : (s + 1) * 128, :] = jnp.broadcast_to(u[s : s + 1, :], (128, 128)).T.astype(BF16)
    W = 512
    for o in range(NO):
        for h in range(KO // W):

            def body(j, acc):
                at = pl.ds(pl.multiple_of(j * 128, 128), 128)
                uu = ucol[at, :]
                prod = gs[o][at, h * W : (h + 1) * W] * jnp.concatenate([uu] * (W // 128), axis=1)
                prod = prod[0:64] + prod[64:128]
                prod = (prod[0:32] + prod[32:64]).astype(F32)
                return acc + ((prod[0:8] + prod[8:16]) + (prod[16:24] + prod[24:32]))

            acc = lax.fori_loop(0, T // 128, body, jnp.zeros((8, W), F32), unroll=8)
            tot = jnp.sum(acc, axis=0, keepdims=True)
            row = (o * KO + h * W) // 128
            rows = jnp.concatenate(
                [tot[:, q * 128 : (q + 1) * 128] for q in range(W // 128)], axis=0
            ).astype(BF16)
            for d in range(ND):
                out[d, row : row + W // 128, :] = rows
    uflat = jnp.concatenate([u[s : s + 1, :] for s in range(NC)], axis=1)
    uhi, ulo = split(uflat)
    us = mm(jnp.concatenate([uhi, ulo, jnp.zeros((6, T), BF16)], axis=0), p_in[...], NT)
    us = column(us[0:1, :] + us[1:2, :])
    xs = xs_in[...].astype(F32)
    aff = jnp.sum(xs * cs_in[...].astype(F32), axis=1, keepdims=True)
    w = (CENTROIDS * jnp.exp2(aff * SCALE)) * us
    w_out[...] = w
    rows = (w * xs).astype(BF16)
    for d in range(ND):
        out[d, 64:320, :] = rows
        out[d, 320:352, :] = ids_in[...]


def potentials(rec, target, vbuf):
    tot = rec[0, 0:64, :].astype(F32)
    for d in range(1, ND):
        tot = tot + rec[d, 0:64, :].astype(F32)
    v = target[...] * (TOKENS / CENTROIDS) / tot
    vbuf[...] = v
    ids = rec[0, 320:352, :].astype(F32)
    for d in range(1, ND):
        ids = ids + rec[d, 320:352, :].astype(F32)
    hi = jnp.concatenate([ids[0:8], ids[16:24]], axis=1)
    lo = jnp.concatenate([ids[8:16], ids[24:32]], axis=1)
    return hi * 32.0 + lo


def own_masses(vbuf, code_in, w):
    code = code_in[0:1, :]
    lid = (code - 1.0).astype(jnp.int32)
    lid = jnp.where(code > 0.0, lid, 0)
    owner = iota((1, SL), 1) >> 5
    row = owner * 8 + (lid >> 7)
    oh = jnp.where(iota((128, SL), 0) == (lid & 127), 1.0, 0.0).astype(BF16)
    vhi, vlo = split(vbuf[...])
    got = mm(vhi, oh) + mm(vlo, oh)
    got = jnp.sum(jnp.where(iota((64, SL), 0) == row, got, 0.0), axis=0, keepdims=True)
    return w * column(got)


def slot_potentials(o, codes, vbuf):
    pos = (codes[o : o + 1, :] - 1.0).astype(jnp.int32)
    vhi, vlo = split(vbuf[o * 8 : (o + 1) * 8, :])
    oh = jnp.where(iota((128, 256), 0) == (pos & 127), 1.0, 0.0).astype(BF16)
    got = mm(vhi, oh) + mm(vlo, oh)
    vs = jnp.sum(jnp.where(iota((8, 256), 0) == (pos >> 7), got, 0.0), axis=0, keepdims=True)
    return pos, vs


def slot_rows(o, rec):
    return jnp.concatenate([rec[d, 64 + o * 32 : 96 + o * 32, :] for d in range(ND)], axis=0)


def refine(o, rec, codes, vbuf, old, new):
    pos, vs = slot_potentials(o, codes, vbuf)
    rows = slot_rows(o, rec)
    for q in range(KO // 256):
        oht = jnp.where(iota((256, 256), 0) + q * 256 == pos, vs, 0.0).astype(BF16)
        at = slice(o * KO + q * 256, o * KO + (q + 1) * 256)
        z = old[at, :].astype(F32) + mm(oht, rows)
        new[at, :] = unit(z).astype(BF16)


def second_kernel(rec, target, code_in, col_in, w_in, old, pay, *refs):
    new, gs, row_out, mass_out, cs_out = refs[0], refs[1 : 1 + NO], refs[1 + NO], refs[2 + NO], refs[3 + NO]
    x, acc, vbuf = refs[4 + NO :]
    for s in range(NC):
        x[s * TOK : (s + 1) * TOK, :] = pay[s, 0:TOK, :]
    codes = potentials(rec, target, vbuf)
    mass_out[...] = own_masses(vbuf, code_in, w_in[...])
    col = col_in[...]
    for o in range(NO):
        refine(o, rec, codes, vbuf, old, new)
    for o in range(NO):
        cblk = new.at[o * KO : (o + 1) * KO]
        cs_out[o * 32 : (o + 1) * 32, :] = mm(owner_onehot(col, o), cblk[...]).astype(BF16)
        vrow = jnp.concatenate([vbuf[o * 8 + q : o * 8 + q + 1, :] for q in range(8)], axis=1)
        score_block(x, cblk, gs[o], acc, vrow, o == 0)
    finish_rows(acc, row_out)


def tail_kernel(rec, target, code_in, col_in, xs_in, cs_in, w_in, mass1, out, vbuf):
    codes = potentials(rec, target, vbuf)
    mass2 = own_masses(vbuf, code_in, w_in[...])
    lane = iota((SL, 128), 1)
    m = jnp.where(lane == 0, mass1[...], jnp.where(lane == 1, mass2, 0.0))
    col = col_in[...]
    new = []
    for o in range(NO):
        pos, vs = slot_potentials(o, codes, vbuf)
        mine = col[o * 32 : (o + 1) * 32, :] - 1.0
        mine = jnp.concatenate([mine, mine], axis=1).astype(jnp.int32)
        oht = jnp.where(mine == pos, vs, 0.0).astype(BF16)
        z = cs_in[o * 32 : (o + 1) * 32, :].astype(F32) + mm(oht, slot_rows(o, rec))
        new.append(unit(z).astype(BF16).astype(F32))
    r = xs_in[...].astype(F32) - jnp.concatenate(new, axis=0)
    i, j = iota((SL, SL), 0), iota((SL, SL), 1)
    want = ((i >> 1) & 7) * 32 + (i >> 4) * 2 + (i & 1)
    perm = jnp.where(j == want, 1.0, 0.0).astype(BF16)
    r = mm(perm, r.astype(BF16)).astype(BF16)
    m = mm(perm, m.astype(BF16)).astype(BF16)
    for s in range(NC):
        out[s, 0:16, :] = r[s * 16 : (s + 1) * 16]
        out[s, 16:32, :] = m[s * 16 : (s + 1) * 16]


def last_kernel(rec, target, old, new, vbuf):
    codes = potentials(rec, target, vbuf)
    for o in range(NO):
        refine(o, rec, codes, vbuf, old, new)


def exchange(x, axis):
    return lax.all_to_all(x, axis, 0, 0, tiled=True)


def on_device(embeddings, centroids, col_mass, assignments):
    target = col_mass.reshape(KC // 128, 128)
    gshape = tuple(pltpu.VMEM((T, KO), BF16) for _ in range(NO))
    sums = shape(NC, NC, 128)
    xacc = (pltpu.VMEM((T, D), BF16), pltpu.VMEM((T, 128), F32))
    vbuf = (pltpu.VMEM((KC // 128, 128), F32),)
    pay = call(pack_kernel, shape(NC, TOK + 16, 128, dtype=BF16), "pack", 10**6, 8)(
        embeddings, assignments
    )
    rec = exchange(pay, "cent")
    c0 = call(cent_kernel, shape(KC, D, dtype=BF16), "cents", 10**9, 12)(centroids)
    def slots(it, *args):
        def body(*refs):
            slot_kernel(it, *refs)

        outs = (
            shape(SL, T, dtype=BF16),
            shape(SL, D, dtype=BF16),
            shape(32, 128, dtype=BF16),
            shape(8, SL),
            shape(SL, 128),
        )
        if it == 0:
            outs += (shape(SL, D, dtype=BF16),)
        return call(body, outs, f"slots{it}", 10**9, 16)(*args)

    def columns(it, rows, p, xs, ids, cs, g):
        out, w = call(
            colsum_kernel,
            (shape(ND, 352, 128, dtype=BF16), shape(SL, 128)),
            f"columns{it}",
            10**9,
            12,
            (pltpu.VMEM((T, 128), BF16),),
        )(rows, p, xs, ids, cs, *g)
        return out, w

    p, xs, ids, code, col0, cs = slots(0, rec, c0)
    rec, c0, xs = lax.optimization_barrier((rec, c0, xs))
    *g, rows = call(first_kernel, gshape + (sums,), "first", 10**10, 12, xacc)(rec, c0)
    rows = exchange(rows, "cent")
    got, w = columns(0, rows, p, xs, ids, cs, g)
    rec, got, w = lax.optimization_barrier((rec, got, w))
    got = exchange(got, "dp")
    p, xs, ids, code1, col = slots(1, rec)
    c1, *rest = call(
        second_kernel,
        (shape(KC, D, dtype=BF16),) + gshape + (sums, shape(SL, 128), shape(SL, D, dtype=BF16)),
        "second",
        10**10,
        12,
        xacc + vbuf,
    )(got, target, code, col, w, c0, rec)
    g, (rows, mass1, cs) = rest[:NO], rest[NO:]
    rows = exchange(rows, "cent")
    got, w = columns(1, rows, p, xs, ids, cs, g)
    got = exchange(got, "dp")
    out = call(tail_kernel, shape(NC, 32, 128, dtype=BF16), "tail", 10**8, 14, vbuf)(
        got, target, code1, col, xs, cs, w, mass1
    )
    got, out = lax.optimization_barrier((got, out))
    back = exchange(out, "cent")
    c2 = call(last_kernel, shape(KC, D, dtype=BF16), "last", 10**9, 14, vbuf)(got, target, c1)
    mass, res = call(unpack_kernel, (shape(2, TOK), shape(TOK, D, dtype=BF16)), "unpack", 10**6, 8)(
        assignments, back
    )
    return c2, mass, res


def solution(mesh):
    in_specs = (P(("dp", "cent"), None), P("cent", None), P("cent"), P(None, ("dp", "cent")))
    out_specs = (P("cent", None), P(None, ("dp", "cent")), P(("dp", "cent"), None))
    return jax.shard_map(
        on_device, mesh=mesh, in_specs=in_specs, out_specs=out_specs, check_vma=False
    )
```

```python
import math

import jax
import jax.numpy as jnp
from jax import lax
from jax.experimental import pallas as pl
from jax.experimental.pallas import tpu as pltpu
from jax.sharding import PartitionSpec as P

F32, BF16 = jnp.float32, jnp.bfloat16
D = 128
TOK = 128
NC, ND = 16, 8
T = TOK * NC
KC = 8192
NO, KO = 8, 1024
SL = 256
SCALE = 20.0 * math.log2(math.e)
TOKENS, CENTROIDS = 16384, 131072
KW = 256
MIB = 2**20

NN = (((1,), (0,)), ((), ()))
NT = (((1,), (1,)), ((), ()))


def mm(a, b, dims=NN):
    return lax.dot_general(a, b, dims, preferred_element_type=F32)


def iota(shape, dim):
    return lax.broadcasted_iota(jnp.int32, shape, dim)


def unit(z):
    return z * lax.rsqrt(jnp.sum(z * z, axis=1, keepdims=True) + 1e-06)


def split(z):
    hi = z.astype(BF16)
    return hi, (z - hi.astype(F32)).astype(BF16)


def column(row):
    return jnp.concatenate(
        [
            jnp.broadcast_to(row[:, i : i + 128], (128, 128)).T
            for i in range(0, row.shape[1], 128)
        ],
        axis=0,
    )


def call(body, outs, name, flops, limit, scratch=()):
    return pl.pallas_call(
        body,
        out_shape=outs,
        scratch_shapes=list(scratch),
        name=name,
        compiler_params=pltpu.CompilerParams(vmem_limit_bytes=limit * MIB),
        cost_estimate=pl.CostEstimate(
            flops=flops, bytes_accessed=2 * MIB, transcendentals=0
        ),
    )


def shape(*dims, dtype=F32):
    return jax.ShapeDtypeStruct(dims, dtype)


def pack_kernel(emb, asg, out):
    xn = unit(emb[...].astype(F32)).astype(BF16)
    rows = []
    for it in range(2):
        a = asg[it : it + 1, :]
        owner = a >> 10
        own_f = owner.astype(F32)
        same = jnp.broadcast_to(own_f, (TOK, TOK)).T == own_f
        before = iota((TOK, TOK), 0) < iota((TOK, TOK), 1)
        rank = jnp.sum(jnp.where(same & before, 1.0, 0.0), axis=0, keepdims=True)
        code = (a & (KO - 1)) + 1
        rows.append((a >> 13, code >> 5, code & 31, (owner & 7) * 2 + rank.astype(jnp.int32)))
    zero = jnp.zeros((5, TOK), jnp.int32)
    for c in range(NC):
        out[c, 0:TOK, :] = xn
        parts = []
        for shard, hi, lo, place in rows:
            mine = shard == c
            parts += [jnp.where(mine, hi, 0), jnp.where(mine, lo, 0), place, zero]
        out[c, TOK : TOK + 16, :] = jnp.concatenate(parts, axis=0).astype(F32).astype(BF16)


def unpack_kernel(asg, rec, mass_out, res_out):
    masses = []
    for it in range(2):
        a = asg[it : it + 1, :]
        owner = a >> 10
        own_f = owner.astype(F32)
        same = jnp.broadcast_to(own_f, (TOK, TOK)).T == own_f
        before = iota((TOK, TOK), 0) < iota((TOK, TOK), 1)
        rank = jnp.sum(jnp.where(same & before, 1.0, 0.0), axis=0, keepdims=True)
        place = (owner.astype(F32) * 2.0 + rank) * 1.0
        shard = a >> 13
        row = shard.astype(F32) * 16.0 + (owner & 7).astype(F32) * 2.0 + rank
        col = column(row)
        lane = iota((TOK, 128), 1).astype(F32)
        oh = jnp.concatenate(
            [jnp.where(col == lane + 128.0 * j, 1.0, 0.0) for j in range(2)], axis=1
        ).astype(BF16)
        mrows = jnp.concatenate([rec[s, 16:32, :] for s in range(NC)], axis=0)
        m = mm(oh, mrows)
        masses.append(m.T[it : it + 1, :])
        if it == 1:
            rrows = jnp.concatenate([rec[s, 0:16, :] for s in range(NC)], axis=0)
            res_out[...] = mm(oh, rrows).astype(BF16)
    mass_out[...] = jnp.concatenate(masses, axis=0)


def cent_kernel(cent, out):
    @pl.loop(0, KC // 256)
    def _(i):
        at = pl.ds(pl.multiple_of(i * 256, 256), 256)
        out[at, :] = unit(cent[at, :].astype(F32)).astype(BF16)


def score_rows(rec, x):
    for s in range(NC):
        hi, lo = split(rec[s, 0:TOK, :].astype(F32) * SCALE)
        x[s * TOK : (s + 1) * TOK, :] = jnp.concatenate([hi, lo], axis=1)


def score_block(x, cblk, g, acc, shift, first):
    part = None
    for k in range(0, KO, KW):
        c = cblk[k : k + KW, :]
        e = mm(x[...], jnp.concatenate([c, c], axis=1), NT)
        if shift is not None:
            e = e + shift[:, k : k + KW]
        e = jnp.exp2(e)
        g[:, k : k + KW] = e.astype(BF16)
        for q in range(0, KW, 128):
            t = e[:, q : q + 128]
            part = t if part is None else part + t
    if first:
        acc[...] = part
    else:
        acc[...] += part


def finish_rows(acc, out):
    hi, lo = split(acc[...])
    one = jnp.ones((8, 128), BF16)
    r = mm(one, hi, NT) + mm(one, lo, NT)
    r = jnp.concatenate([r[0:1, s * 128 : (s + 1) * 128] for s in range(NC)], axis=0)
    for c in range(NC):
        out[c] = r


def first_kernel(rec, cents, *refs):
    gs, row_out, x, acc = refs[:NO], refs[NO], refs[NO + 1], refs[NO + 2]
    score_rows(rec, x)
    for o in range(NO):
        score_block(x, cents.at[o * KO : (o + 1) * KO], gs[o], acc, None, o == 0)
    finish_rows(acc, row_out)


def owner_onehot(idcol, o):
    ids = idcol[o * 32 : (o + 1) * 32, :]
    lane = iota((32, 128), 1).astype(F32)
    return jnp.concatenate(
        [jnp.where(ids == lane + (128.0 * j + 1.0), 1.0, 0.0) for j in range(KO // 128)],
        axis=1,
    ).astype(BF16)


def order_matrix(back):
    i, j = iota((SL, SL), 0), iota((SL, SL), 1)
    if back:
        want = ((i >> 1) & 7) * 32 + (i >> 4) * 2 + (i & 1)
    else:
        want = ((i >> 1) & 15) * 16 + (i >> 5) * 2 + (i & 1)
    return jnp.where(j == want, 1.0, 0.0).astype(BF16)


def slot_kernel(rec, cents, p_out, xs_out, id_out, code_out, col_out, cs_out):
    me = lax.axis_index("dp")
    order = order_matrix(False)
    for it in range(2):
        base = TOK + 8 * it
        place16 = iota((16, TOK), 0).astype(F32)
        xs, digits = [], []
        for s in range(NC):
            meta = rec[s, base : base + 8, :].astype(F32)
            hi, lo, place = meta[0:1, :], meta[1:2, :], meta[2:3, :]
            p = jnp.where((place16 == place) & (hi + lo > 0.0), 1.0, 0.0)
            p_out[it, s * 16 : (s + 1) * 16, :] = p
            xs.append(mm(p.astype(BF16), rec[s, 0:TOK, :]))
            digits.append(
                jnp.concatenate(
                    [
                        jnp.broadcast_to(jnp.sum(p * q, axis=1, keepdims=True), (16, 128))
                        for q in (hi, lo)
                    ],
                    axis=1,
                )
            )
        both = jnp.concatenate([jnp.concatenate(xs, axis=0), jnp.concatenate(digits, axis=0)], axis=1)
        both = mm(order, both.astype(BF16))
        xs_out[it] = both[:, 0:128].astype(BF16)
        dhi, dlo = both[:, 128:256], both[:, 256:384]
        col = dhi * 32.0 + dlo
        col_out[it] = col
        rhi = jnp.concatenate([dhi[0:128].T[0:1], dhi[128:256].T[0:1]], axis=1)
        rlo = jnp.concatenate([dlo[0:128].T[0:1], dlo[128:256].T[0:1]], axis=1)
        code_out[it] = jnp.broadcast_to(rhi * 32.0 + rlo, (8, SL))
        slot = iota((SL, SL), 0)
        lane = jnp.where(iota((SL, SL), 1) == me * 32 + (slot & 31), 1.0, 0.0).astype(BF16)
        own = iota((8, SL), 0) == (iota((8, SL), 1) >> 5)
        rows = jnp.concatenate([jnp.where(own, rhi, 0.0), jnp.where(own, rlo, 0.0)], axis=0)
        ids = mm(rows.astype(BF16), lane)
        id_out[it] = jnp.concatenate([ids[:, 0:128], ids[:, 128:256]], axis=0).astype(BF16)
        if it == 0:
            for o in range(NO):
                cs_out[o * 32 : (o + 1) * 32, :] = mm(
                    owner_onehot(col, o), cents[o * KO : (o + 1) * KO, :]
                ).astype(BF16)


def colsum_kernel(it, rowp, p_in, xs_in, ids_in, cs_in, *refs):
    gs, out, w_out, ucol, tots = refs[:NO], refs[NO], refs[NO + 1], refs[NO + 2], refs[NO + 3]
    u = 1.0 / jnp.sum(rowp[...], axis=0)
    for s in range(NC):
        ucol[s * 128 : (s + 1) * 128, :] = jnp.broadcast_to(u[s : s + 1, :], (128, 128)).T.astype(BF16)
    W = 512
    for o in range(NO):
        for h in range(KO // W):

            def body(j, acc):
                at = pl.ds(pl.multiple_of(j * 128, 128), 128)
                uu = ucol[at, :]
                prod = gs[o][at, h * W : (h + 1) * W] * jnp.concatenate([uu] * (W // 128), axis=1)
                prod = prod[0:64] + prod[64:128]
                prod = (prod[0:32] + prod[32:64]).astype(F32)
                return acc + ((prod[0:8] + prod[8:16]) + (prod[16:24] + prod[24:32]))

            acc = lax.fori_loop(0, T // 128, body, jnp.zeros((8, W), F32), unroll=8)
            tot = jnp.sum(acc, axis=0, keepdims=True)
            row = (o * KO + h * W) // 128
            for q in range(W // 128):
                tots[row + q : row + q + 1, :] = tot[:, q * 128 : (q + 1) * 128]
    us = jnp.concatenate(
        [
            jnp.sum(p_in[it, s * 16 : (s + 1) * 16, :] * u[s : s + 1, :], axis=1, keepdims=True)
            for s in range(NC)
        ],
        axis=0,
    )
    uhi, ulo = split(jnp.broadcast_to(us, (SL, 128)))
    both = mm(order_matrix(False), jnp.concatenate([uhi, ulo], axis=1))
    us = both[:, 0:128] + both[:, 128:256]
    xs = xs_in[it].astype(F32)
    aff = jnp.sum(xs * cs_in[...].astype(F32), axis=1, keepdims=True)
    w = (CENTROIDS * jnp.exp2(aff * SCALE)) * us
    w_out[...] = w
    rows = (w * xs).astype(BF16)
    tot = tots[...].astype(BF16)
    for d in range(ND):
        out[d, 0:64, :] = tot
        out[d, 64:320, :] = rows
        out[d, 320:352, :] = ids_in[it]


def potentials(rec, target, vbuf, before=None):
    tot = rec[0, 0:64, :].astype(F32)
    for d in range(1, ND):
        tot = tot + rec[d, 0:64, :].astype(F32)
    v = target[...] * (TOKENS / CENTROIDS) / tot
    if before is not None:
        v = v * before[...]
    vbuf[...] = v
    ids = rec[0, 320:352, :].astype(F32)
    for d in range(1, ND):
        ids = ids + rec[d, 320:352, :].astype(F32)
    hi = jnp.concatenate([ids[0:8], ids[16:24]], axis=1)
    lo = jnp.concatenate([ids[8:16], ids[24:32]], axis=1)
    return hi * 32.0 + lo


def own_masses(vbuf, code_in, it, w):
    code = code_in[it][0:1, :]
    lid = (code - 1.0).astype(jnp.int32)
    lid = jnp.where(code > 0.0, lid, 0)
    owner = iota((1, SL), 1) >> 5
    row = owner * 8 + (lid >> 7)
    oh = jnp.where(iota((128, SL), 0) == (lid & 127), 1.0, 0.0).astype(BF16)
    vhi, vlo = split(vbuf[...])
    got = mm(vhi, oh) + mm(vlo, oh)
    got = jnp.sum(jnp.where(iota((64, SL), 0) == row, got, 0.0), axis=0, keepdims=True)
    return w * column(got)


def slot_potentials(o, codes, vbuf):
    pos = (codes[o : o + 1, :] - 1.0).astype(jnp.int32)
    vhi, vlo = split(vbuf[o * 8 : (o + 1) * 8, :])
    oh = jnp.where(iota((128, 256), 0) == (pos & 127), 1.0, 0.0).astype(BF16)
    got = mm(vhi, oh) + mm(vlo, oh)
    vs = jnp.sum(jnp.where(iota((8, 256), 0) == (pos >> 7), got, 0.0), axis=0, keepdims=True)
    return pos, vs


def slot_rows(o, rec):
    return jnp.concatenate([rec[d, 64 + o * 32 : 96 + o * 32, :] for d in range(ND)], axis=0)


def refine(o, rec, codes, vbuf, old, new):
    pos, vs = slot_potentials(o, codes, vbuf)
    rows = slot_rows(o, rec)
    oht = jnp.where(iota((KO, 256), 0) == pos, vs, 0.0).astype(BF16)
    at = slice(o * KO, (o + 1) * KO)
    z = old[at, :].astype(F32) + mm(oht, rows)
    new[at, :] = unit(z).astype(BF16)


def second_kernel(rec, target, code_in, col_in, w_in, old, pay, *refs):
    new, gs, row_out, mass_out, cs_out, v_out = refs[0], refs[1 : 1 + NO], *refs[1 + NO : 5 + NO]
    x, acc, vbuf = refs[5 + NO :]
    score_rows(pay, x)
    codes = potentials(rec, target, vbuf)
    v_out[...] = vbuf[...]
    logv = jnp.log2(vbuf[...])
    mass_out[...] = own_masses(vbuf, code_in, 0, w_in[...])
    col = col_in[1]
    for o in range(NO):
        refine(o, rec, codes, vbuf, old, new)
    for o in range(NO):
        cblk = new.at[o * KO : (o + 1) * KO]
        cs_out[o * 32 : (o + 1) * 32, :] = mm(owner_onehot(col, o), cblk[...]).astype(BF16)
        shift = jnp.concatenate([logv[o * 8 + q : o * 8 + q + 1, :] for q in range(8)], axis=1)
        score_block(x, cblk, gs[o], acc, shift, o == 0)
    finish_rows(acc, row_out)


def tail_kernel(rec, target, v_in, code_in, col_in, xs_in, cs_in, w_in, mass1, out, vbuf):
    codes = potentials(rec, target, vbuf, v_in)
    mass2 = own_masses(vbuf, code_in, 1, w_in[...])
    lane = iota((SL, 128), 1)
    m = jnp.where(lane == 0, mass1[...], jnp.where(lane == 1, mass2, 0.0))
    col = col_in[1]
    new = []
    for o in range(NO):
        pos, vs = slot_potentials(o, codes, vbuf)
        mine = col[o * 32 : (o + 1) * 32, :] - 1.0
        mine = jnp.concatenate([mine, mine], axis=1).astype(jnp.int32)
        oht = jnp.where(mine == pos, vs, 0.0).astype(BF16)
        z = cs_in[o * 32 : (o + 1) * 32, :].astype(F32) + mm(oht, slot_rows(o, rec))
        new.append(unit(z).astype(BF16).astype(F32))
    r = xs_in[1].astype(F32) - jnp.concatenate(new, axis=0)
    perm = order_matrix(True)
    r = mm(perm, r.astype(BF16)).astype(BF16)
    m = mm(perm, m.astype(BF16)).astype(BF16)
    for s in range(NC):
        out[s, 0:16, :] = r[s * 16 : (s + 1) * 16]
        out[s, 16:32, :] = m[s * 16 : (s + 1) * 16]


def last_kernel(rec, target, v_in, old, new, vbuf):
    codes = potentials(rec, target, vbuf, v_in)
    for o in range(NO):
        refine(o, rec, codes, vbuf, old, new)


def exchange(x, axis):
    return lax.all_to_all(x, axis, 0, 0, tiled=True)


def on_device(embeddings, centroids, col_mass, assignments):
    target = col_mass.reshape(KC // 128, 128)
    gshape = tuple(pltpu.VMEM((T, KO), BF16) for _ in range(NO))
    sums = shape(NC, NC, 128)
    xacc = (pltpu.VMEM((T, 2 * D), BF16), pltpu.VMEM((T, 128), F32))
    vbuf = (pltpu.VMEM((KC // 128, 128), F32),)
    pay = call(pack_kernel, shape(NC, TOK + 16, 128, dtype=BF16), "pack", 10**6, 8)(
        embeddings, assignments
    )
    rec = exchange(pay, "cent")
    c0 = call(cent_kernel, shape(KC, D, dtype=BF16), "cents", 10**9, 12)(centroids)
    p, xs, ids, code, col, cs = call(
        slot_kernel,
        (
            shape(2, SL, TOK),
            shape(2, SL, D, dtype=BF16),
            shape(2, 32, 128, dtype=BF16),
            shape(2, 8, SL),
            shape(2, SL, 128),
            shape(SL, D, dtype=BF16),
        ),
        "slots",
        10**9,
        12,
    )(rec, c0)
    rec, c0, xs = lax.optimization_barrier((rec, c0, xs))

    def columns(it, rows, cs, g):
        def body(*refs):
            colsum_kernel(it, *refs)

        out, w = call(
            body,
            (shape(ND, 352, 128, dtype=BF16), shape(SL, 128)),
            f"columns{it}",
            10**9,
            12,
            (pltpu.VMEM((T, 128), BF16), pltpu.VMEM((64, 128), F32)),
        )(rows, p, xs, ids, cs, *g)
        return exchange(out, "dp"), w

    *g, rows = call(first_kernel, gshape + (sums,), "first", 10**10, 12, xacc)(rec, c0)
    rows = exchange(rows, "cent")
    got, w = columns(0, rows, cs, g)
    c1, *rest = call(
        second_kernel,
        (shape(KC, D, dtype=BF16),) + gshape
        + (sums, shape(SL, 128), shape(SL, D, dtype=BF16), shape(KC // 128, 128)),
        "second",
        10**10,
        12,
        xacc + vbuf,
    )(got, target, code, col, w, c0, rec)
    g, (rows, mass1, cs, v1) = rest[:NO], rest[NO:]
    rows = exchange(rows, "cent")
    got, w = columns(1, rows, cs, g)
    out = call(tail_kernel, shape(NC, 32, 128, dtype=BF16), "tail", 10**8, 14, vbuf)(
        got, target, v1, code, col, xs, cs, w, mass1
    )
    got, out = lax.optimization_barrier((got, out))
    back = exchange(out, "cent")
    c2 = call(last_kernel, shape(KC, D, dtype=BF16), "last", 10**9, 14, vbuf)(got, target, v1, c1)
    mass, res = call(unpack_kernel, (shape(2, TOK), shape(TOK, D, dtype=BF16)), "unpack", 10**6, 8)(
        assignments, back
    )
    return c2, mass, res


def solution(mesh):
    in_specs = (P(("dp", "cent"), None), P("cent", None), P("cent"), P(None, ("dp", "cent")))
    out_specs = (P("cent", None), P(None, ("dp", "cent")), P(("dp", "cent"), None))
    return jax.shard_map(
        on_device, mesh=mesh, in_specs=in_specs, out_specs=out_specs, check_vma=False
    )
```

```python
import math

import jax
import jax.numpy as jnp
from jax import lax
from jax.experimental import pallas as pl
from jax.experimental.pallas import tpu as pltpu
from jax.sharding import PartitionSpec as P

F32, BF16 = jnp.float32, jnp.bfloat16
D = 128
TOK = 128
NC, ND = 16, 8
T = TOK * NC
KC = 8192
NO, KO = 8, 1024
SL = 256
SCALE = 20.0 * math.log2(math.e)
TOKENS, CENTROIDS = 16384, 131072
KW = 256
MIB = 2**20

NN = (((1,), (0,)), ((), ()))
NT = (((1,), (1,)), ((), ()))


def mm(a, b, dims=NN):
    return lax.dot_general(a, b, dims, preferred_element_type=F32)


def iota(shape, dim):
    return lax.broadcasted_iota(jnp.int32, shape, dim)


def unit(z):
    return z * lax.rsqrt(jnp.sum(z * z, axis=1, keepdims=True) + 1e-06)


def split(z):
    hi = z.astype(BF16)
    return hi, (z - hi.astype(F32)).astype(BF16)


def column(row):
    return jnp.concatenate(
        [
            jnp.broadcast_to(row[:, i : i + 128], (128, 128)).T
            for i in range(0, row.shape[1], 128)
        ],
        axis=0,
    )


def call(body, outs, name, flops, limit, scratch=(), **specs):
    return pl.pallas_call(
        body,
        **specs,
        out_shape=outs,
        scratch_shapes=list(scratch),
        name=name,
        compiler_params=pltpu.CompilerParams(vmem_limit_bytes=limit * MIB),
        cost_estimate=pl.CostEstimate(
            flops=flops, bytes_accessed=2 * MIB, transcendentals=0
        ),
    )


def shape(*dims, dtype=F32):
    return jax.ShapeDtypeStruct(dims, dtype)


def pack_kernel(emb_hbm, asg_hbm, out, emb, asg, sems):
    copies = [
        pltpu.make_async_copy(emb_hbm, emb, sems.at[0]),
        pltpu.make_async_copy(asg_hbm, asg, sems.at[1]),
    ]
    for c in copies:
        c.start()
    for c in copies:
        c.wait()
    xn = unit(emb[...].astype(F32)).astype(BF16)
    rows = []
    for it in range(2):
        a = asg[it : it + 1, :]
        owner = a >> 10
        own_f = owner.astype(F32)
        same = jnp.broadcast_to(own_f, (TOK, TOK)).T == own_f
        before = iota((TOK, TOK), 0) < iota((TOK, TOK), 1)
        rank = jnp.sum(jnp.where(same & before, 1.0, 0.0), axis=0, keepdims=True)
        code = (a & (KO - 1)) + 1
        rows.append((a >> 13, code >> 5, code & 31, (owner & 7) * 2 + rank.astype(jnp.int32)))
    zero = jnp.zeros((5, TOK), jnp.int32)
    for c in range(NC):
        out[c, 0:TOK, :] = xn
        parts = []
        for shard, hi, lo, place in rows:
            mine = shard == c
            parts += [jnp.where(mine, hi, 0), jnp.where(mine, lo, 0), place, zero]
        out[c, TOK : TOK + 16, :] = jnp.concatenate(parts, axis=0).astype(F32).astype(BF16)


def unpack_kernel(asg, rec, mass_out, res_out):
    masses = []
    for it in range(2):
        a = asg[it : it + 1, :]
        owner = a >> 10
        own_f = owner.astype(F32)
        same = jnp.broadcast_to(own_f, (TOK, TOK)).T == own_f
        before = iota((TOK, TOK), 0) < iota((TOK, TOK), 1)
        rank = jnp.sum(jnp.where(same & before, 1.0, 0.0), axis=0, keepdims=True)
        place = (owner.astype(F32) * 2.0 + rank) * 1.0
        shard = a >> 13
        row = shard.astype(F32) * 16.0 + (owner & 7).astype(F32) * 2.0 + rank
        col = column(row)
        lane = iota((TOK, 128), 1).astype(F32)
        oh = jnp.concatenate(
            [jnp.where(col == lane + 128.0 * j, 1.0, 0.0) for j in range(2)], axis=1
        ).astype(BF16)
        mrows = jnp.concatenate([rec[s, 16:32, :] for s in range(NC)], axis=0)
        m = mm(oh, mrows)
        masses.append(m.T[it : it + 1, :])
        if it == 1:
            rrows = jnp.concatenate([rec[s, 0:16, :] for s in range(NC)], axis=0)
            res_out[...] = mm(oh, rrows).astype(BF16)
    mass_out[...] = jnp.concatenate(masses, axis=0)


def cent_kernel(cent, out):
    @pl.loop(0, KC // 256)
    def _(i):
        at = pl.ds(pl.multiple_of(i * 256, 256), 256)
        out[at, :] = unit(cent[at, :].astype(F32)).astype(BF16)


def score_rows(rec, x):
    for s in range(NC):
        hi, lo = split(rec[s, 0:TOK, :].astype(F32) * SCALE)
        x[s * TOK : (s + 1) * TOK, :] = jnp.concatenate([hi, lo], axis=1)


def score_block(x, cblk, g, acc, shift, first):
    part = None
    for k in range(0, KO, KW):
        c = cblk[k : k + KW, :]
        e = mm(x[...], jnp.concatenate([c, c], axis=1), NT)
        if shift is not None:
            e = e + shift[:, k : k + KW]
        e = jnp.exp2(e)
        g[:, k : k + KW] = e.astype(BF16)
        for q in range(0, KW, 128):
            t = e[:, q : q + 128]
            part = t if part is None else part + t
    if first:
        acc[...] = part
    else:
        acc[...] += part


def finish_rows(acc, out):
    hi, lo = split(acc[...])
    one = jnp.ones((8, 128), BF16)
    r = mm(one, hi, NT) + mm(one, lo, NT)
    r = jnp.concatenate([r[0:1, s * 128 : (s + 1) * 128] for s in range(NC)], axis=0)
    for c in range(NC):
        out[c] = r


def first_kernel(rec, cents, *refs):
    gs, row_out, x, acc = refs[:NO], refs[NO], refs[NO + 1], refs[NO + 2]
    score_rows(rec, x)
    for o in range(NO):
        score_block(x, cents.at[o * KO : (o + 1) * KO], gs[o], acc, None, o == 0)
    finish_rows(acc, row_out)


def owner_onehot(idcol, o):
    ids = idcol[o * 32 : (o + 1) * 32, :]
    lane = iota((32, 128), 1).astype(F32)
    return jnp.concatenate(
        [jnp.where(ids == lane + (128.0 * j + 1.0), 1.0, 0.0) for j in range(KO // 128)],
        axis=1,
    ).astype(BF16)


def order_matrix(back):
    i, j = iota((SL, SL), 0), iota((SL, SL), 1)
    if back:
        want = ((i >> 1) & 7) * 32 + (i >> 4) * 2 + (i & 1)
    else:
        want = ((i >> 1) & 15) * 16 + (i >> 5) * 2 + (i & 1)
    return jnp.where(j == want, 1.0, 0.0).astype(BF16)


def slot_kernel(rec, cents, p_out, xs_out, id_out, col_out, cs_out):
    order = order_matrix(False)
    for it in range(2):
        base = TOK + 8 * it
        place16 = iota((16, TOK), 0).astype(F32)
        xs, digits = [], []
        for s in range(NC):
            meta = rec[s, base : base + 8, :].astype(F32)
            hi, lo, place = meta[0:1, :], meta[1:2, :], meta[2:3, :]
            p = jnp.where((place16 == place) & (hi + lo > 0.0), 1.0, 0.0)
            p_out[it, s * 16 : (s + 1) * 16, :] = p
            xs.append(mm(p.astype(BF16), rec[s, 0:TOK, :]))
            digits.append(
                jnp.concatenate(
                    [
                        jnp.broadcast_to(jnp.sum(p * q, axis=1, keepdims=True), (16, 128))
                        for q in (hi, lo)
                    ],
                    axis=1,
                )
            )
        both = jnp.concatenate([jnp.concatenate(xs, axis=0), jnp.concatenate(digits, axis=0)], axis=1)
        both = mm(order, both.astype(BF16))
        xs_out[it] = both[:, 0:128].astype(BF16)
        dhi, dlo = both[:, 128:256], both[:, 256:384]
        col = dhi * 32.0 + dlo
        col_out[it] = col
        rhi = jnp.concatenate([dhi[0:128].T[0:1], dhi[128:256].T[0:1]], axis=1)
        rlo = jnp.concatenate([dlo[0:128].T[0:1], dlo[128:256].T[0:1]], axis=1)
        lane = jnp.where(iota((SL, 128), 1) == (iota((SL, 128), 0) & 31), 1.0, 0.0).astype(BF16)
        own = iota((8, SL), 0) == (iota((8, SL), 1) >> 5)
        rows = jnp.concatenate([jnp.where(own, rhi, 0.0), jnp.where(own, rlo, 0.0)], axis=0)
        id_out[it] = mm(rows.astype(BF16), lane).astype(BF16)
        if it == 0:
            for o in range(NO):
                cs_out[o * 32 : (o + 1) * 32, :] = mm(
                    owner_onehot(col, o), cents[o * KO : (o + 1) * KO, :]
                ).astype(BF16)


def colsum_kernel(it, rowp, p_in, xs_in, cs_in, meta, *refs):
    gs, (out, w_out, ucol, tots) = refs[:NO], refs[NO:]
    u = 1.0 / jnp.sum(rowp[...], axis=0)
    for s in range(NC):
        ucol[s * 128 : (s + 1) * 128, :] = jnp.broadcast_to(u[s : s + 1, :], (128, 128)).T.astype(BF16)
    W = 512
    for o in range(NO):
        for h in range(KO // W):

            def body(j, acc):
                at = pl.ds(pl.multiple_of(j * 128, 128), 128)
                uu = ucol[at, :]
                prod = gs[o][at, h * W : (h + 1) * W] * jnp.concatenate([uu] * (W // 128), axis=1)
                prod = prod[0:64] + prod[64:128]
                prod = (prod[0:32] + prod[32:64]).astype(F32)
                return acc + ((prod[0:8] + prod[8:16]) + (prod[16:24] + prod[24:32]))

            acc = lax.fori_loop(0, T // 128, body, jnp.zeros((8, W), F32), unroll=8)
            tot = jnp.sum(acc, axis=0, keepdims=True)
            row = (o * KO + h * W) // 128
            for q in range(W // 128):
                tots[row + q : row + q + 1, :] = tot[:, q * 128 : (q + 1) * 128]
    us = jnp.concatenate(
        [
            jnp.sum(p_in[it, s * 16 : (s + 1) * 16, :] * u[s : s + 1, :], axis=1, keepdims=True)
            for s in range(NC)
        ],
        axis=0,
    )
    uhi, ulo = split(jnp.broadcast_to(us, (SL, 128)))
    both = mm(order_matrix(False), jnp.concatenate([uhi, ulo], axis=1))
    us = both[:, 0:128] + both[:, 128:256]
    xs = xs_in[it].astype(F32)
    aff = jnp.sum(xs * cs_in[...].astype(F32), axis=1, keepdims=True)
    w = (CENTROIDS * jnp.exp2(aff * SCALE)) * us
    w_out[...] = w
    rows = (w * xs).astype(BF16)
    if it == 0:
        tot = tots[...].astype(BF16)
    else:
        got = jnp.concatenate([slot_values(o, meta, tots)[1] for o in range(NO)], axis=0)
        tot = jnp.concatenate([got[:, 0:128], got[:, 128:256]], axis=0).astype(BF16)
    base = tot.shape[0]
    for d in range(ND):
        out[d, 0:base, :] = tot
        out[d, base : base + SL, :] = rows
        if it == 0:
            out[d, 320:336, :] = meta[0]
            out[d, 336:352, :] = meta[1]


def slot_codes(rec, base):
    halves = []
    for h in range(2):
        tot = rec[4 * h, base : base + 16, :].astype(F32)
        for q in range(1, 4):
            tot = tot + pltpu.roll(rec[4 * h + q, base : base + 16, :].astype(F32), 32 * q, 1)
        halves.append(tot)
    both = jnp.concatenate(halves, axis=1)
    return both[0:8] * 32.0 + both[8:16]


def own_row(values):
    at = lax.axis_index("dp") * 32 + (iota((SL, SL), 1) & 31)
    pick = jnp.where(iota((SL, SL), 0) == at, 1.0, 0.0).astype(BF16)
    hi, lo = split(values)
    got = mm(jnp.concatenate([hi, lo], axis=0), pick)
    got = got[0:8] + got[8:16]
    own = iota((8, SL), 0) == (iota((8, SL), 1) >> 5)
    return jnp.sum(jnp.where(own, got, 0.0), axis=0, keepdims=True)


def slot_values(o, codes, table):
    pos = (codes[o : o + 1, :] - 1.0).astype(jnp.int32)
    hi, lo = split(table[o * 8 : (o + 1) * 8, :])
    oh = jnp.where(iota((128, 256), 0) == (pos & 127), 1.0, 0.0).astype(BF16)
    got = mm(jnp.concatenate([hi, lo], axis=0), oh)
    got = got[0:8] + got[8:16]
    val = jnp.sum(jnp.where(iota((8, 256), 0) == (pos >> 7), got, 0.0), axis=0, keepdims=True)
    return pos, val


def slot_rows(o, rec, base):
    return jnp.concatenate(
        [rec[d, base + o * 32 : base + (o + 1) * 32, :] for d in range(ND)], axis=0
    )


def refine(o, pos, vs, rows, old, new):
    oht = jnp.where(iota((KO, 256), 0) == pos, vs, 0.0).astype(BF16)
    at = slice(o * KO, (o + 1) * KO)
    z = old[at, :].astype(F32) + mm(oht, rows)
    new[at, :] = unit(z).astype(BF16)


def second_kernel(rec, target, col_in, w_in, old, pay, *refs):
    gs, (new_hbm, row_out, mass_out, cs_out, code_out, tv_out) = refs[:NO], refs[NO : 6 + NO]
    x, acc, vbuf, new, sem = refs[6 + NO :]
    score_rows(pay, x)
    tot = rec[0, 0:64, :].astype(F32)
    for d in range(1, ND):
        tot = tot + rec[d, 0:64, :].astype(F32)
    goal = target[...] * (TOKENS / CENTROIDS)
    v = goal / tot
    vbuf[...] = v
    logv = jnp.log2(v)
    codes = slot_codes(rec, 320)
    slots = [slot_values(o, codes, vbuf) for o in range(NO)]
    for o in range(NO):
        refine(o, *slots[o], slot_rows(o, rec, 64), old, new)
    save = pltpu.make_async_copy(new, new_hbm, sem)
    save.start()
    vs = jnp.concatenate([val for _, val in slots], axis=0)
    mass_out[...] = w_in[...] * column(own_row(vs))
    codes = slot_codes(rec, 336)
    code_out[...] = codes
    vbuf[...] = goal * v
    tv_out[...] = jnp.concatenate([slot_values(o, codes, vbuf)[1] for o in range(NO)], axis=0)
    col = col_in[1]
    for o in range(NO):
        cblk = new.at[o * KO : (o + 1) * KO]
        cs_out[o * 32 : (o + 1) * 32, :] = mm(owner_onehot(col, o), cblk[...]).astype(BF16)
        shift = jnp.concatenate([logv[o * 8 + q : o * 8 + q + 1, :] for q in range(8)], axis=1)
        score_block(x, cblk, gs[o], acc, shift, o == 0)
    finish_rows(acc, row_out)
    save.wait()


def last_potentials(rec, codes, tv):
    tot = rec[0, 0:16, :].astype(F32)
    for d in range(1, ND):
        tot = tot + rec[d, 0:16, :].astype(F32)
    tot = jnp.concatenate([tot[0:8], tot[8:16]], axis=1)
    some = codes[...] > 0.0
    return jnp.where(some, tv[...] / jnp.where(some, tot, 1.0), 0.0)


def tail_kernel(rec, codes, tv, col_in, xs_in, cs_in, w_in, mass1, out):
    vs = last_potentials(rec, codes, tv)
    mass2 = w_in[...] * column(own_row(vs))
    lane = iota((SL, 128), 1)
    m = jnp.where(lane == 0, mass1[...], jnp.where(lane == 1, mass2, 0.0))
    pos = (codes[...] - 1.0).astype(jnp.int32)
    col = col_in[1]
    new = []
    for o in range(NO):
        mine = col[o * 32 : (o + 1) * 32, :] - 1.0
        mine = jnp.concatenate([mine, mine], axis=1).astype(jnp.int32)
        oht = jnp.where(mine == pos[o : o + 1, :], vs[o : o + 1, :], 0.0).astype(BF16)
        z = cs_in[o * 32 : (o + 1) * 32, :].astype(F32) + mm(oht, slot_rows(o, rec, 16))
        new.append(unit(z).astype(BF16).astype(F32))
    r = xs_in[1].astype(F32) - jnp.concatenate(new, axis=0)
    both = jnp.concatenate([r.astype(BF16), m.astype(BF16)], axis=1)
    both = mm(order_matrix(True), both).astype(BF16)
    for s in range(NC):
        out[s, 0:16, :] = both[s * 16 : (s + 1) * 16, 0:128]
        out[s, 16:32, :] = both[s * 16 : (s + 1) * 16, 128:256]


def last_kernel(rec, codes, tv, old, new):
    vs = last_potentials(rec, codes, tv)
    pos = (codes[...] - 1.0).astype(jnp.int32)
    for o in range(NO):
        refine(o, pos[o : o + 1, :], vs[o : o + 1, :], slot_rows(o, rec, 16), old, new)


def exchange(x, axis):
    return lax.all_to_all(x, axis, 0, 0, tiled=True)


def on_device(embeddings, centroids, col_mass, assignments):
    target = col_mass.reshape(KC // 128, 128)
    gshape = tuple(pltpu.VMEM((T, KO), BF16) for _ in range(NO))
    sums = shape(NC, NC, 128)
    xacc = (pltpu.VMEM((T, 2 * D), BF16), pltpu.VMEM((T, 128), F32))
    pay = call(
        pack_kernel,
        shape(NC, TOK + 16, 128, dtype=BF16),
        "pack",
        10**6,
        8,
        (pltpu.VMEM((TOK, D), BF16), pltpu.VMEM((2, TOK), jnp.int32), pltpu.SemaphoreType.DMA((2,))),
        in_specs=[pl.BlockSpec(memory_space=pl.ANY)] * 2,
    )(embeddings, assignments)
    rec = exchange(pay, "cent")
    c0 = call(cent_kernel, shape(KC, D, dtype=BF16), "cents", 10**9, 12)(centroids)
    p, xs, ids, col, cs = call(
        slot_kernel,
        (
            shape(2, SL, TOK),
            shape(2, SL, D, dtype=BF16),
            shape(2, 16, 128, dtype=BF16),
            shape(2, SL, 128),
            shape(SL, D, dtype=BF16),
        ),
        "slots",
        10**9,
        12,
    )(rec, c0)
    rec, c0, xs = lax.optimization_barrier((rec, c0, xs))

    def columns(it, rows, cs, meta, g):
        def body(*refs):
            colsum_kernel(it, *refs)

        out, w = call(
            body,
            (shape(ND, 272 if it else 352, 128, dtype=BF16), shape(SL, 128)),
            f"columns{it}",
            10**9,
            12,
            (pltpu.VMEM((T, 128), BF16), pltpu.VMEM((64, 128), F32)),
        )(rows, p, xs, cs, meta, *g)
        return exchange(out, "dp"), w

    *g, rows = call(first_kernel, gshape + (sums,), "first", 10**10, 12, xacc)(rec, c0)
    rows = exchange(rows, "cent")
    got, w = columns(0, rows, cs, ids, g)
    vmem = pl.BlockSpec(memory_space=pltpu.VMEM)
    *g, c1, rows, mass1, cs, codes, tv = call(
        second_kernel,
        gshape
        + (
            pltpu.HBM((KC, D), BF16),
            sums,
            shape(SL, 128),
            shape(SL, D, dtype=BF16),
            shape(NO, SL),
            shape(NO, SL),
        ),
        "second",
        10**10,
        12,
        xacc + (pltpu.VMEM((KC // 128, 128), F32), pltpu.VMEM((KC, D), BF16), pltpu.SemaphoreType.DMA),
        out_specs=(vmem,) * NO + (pl.BlockSpec(memory_space=pltpu.HBM),) + (vmem,) * 5,
    )(got, target, col, w, c0, rec)
    rows = exchange(rows, "cent")
    got, w = columns(1, rows, cs, codes, g)
    out = call(tail_kernel, shape(NC, 32, 128, dtype=BF16), "tail", 10**8, 12)(
        got, codes, tv, col, xs, cs, w, mass1
    )
    got, out = lax.optimization_barrier((got, out))
    back = exchange(out, "cent")
    c2 = call(last_kernel, shape(KC, D, dtype=BF16), "last", 10**9, 12)(got, codes, tv, c1)
    mass, res = call(unpack_kernel, (shape(2, TOK), shape(TOK, D, dtype=BF16)), "unpack", 10**6, 8)(
        assignments, back
    )
    return c2, mass, res


def solution(mesh):
    in_specs = (P(("dp", "cent"), None), P("cent", None), P("cent"), P(None, ("dp", "cent")))
    out_specs = (P("cent", None), P(None, ("dp", "cent")), P(("dp", "cent"), None))
    return jax.shard_map(
        on_device, mesh=mesh, in_specs=in_specs, out_specs=out_specs, check_vma=False
    )
```

```python
import math

import jax
import jax.numpy as jnp
from jax import lax
from jax.experimental import pallas as pl
from jax.experimental.pallas import tpu as pltpu
from jax.sharding import PartitionSpec as P

F32, BF16 = jnp.float32, jnp.bfloat16
D = 128
TOK = 128
NC, ND = 16, 8
T = TOK * NC
KC = 8192
NO, KO = 8, 1024
SL = 256
SCALE = 20.0 * math.log2(math.e)
TOKENS, CENTROIDS = 16384, 131072
KW = 256
MIB = 2**20

NN = (((1,), (0,)), ((), ()))
NT = (((1,), (1,)), ((), ()))


def mm(a, b, dims=NN):
    return lax.dot_general(a, b, dims, preferred_element_type=F32)


def iota(shape, dim):
    return lax.broadcasted_iota(jnp.int32, shape, dim)


def unit(z):
    return z * lax.rsqrt(jnp.sum(z * z, axis=1, keepdims=True) + 1e-06)


def split(z):
    hi = z.astype(BF16)
    return hi, (z - hi.astype(F32)).astype(BF16)


def column(row):
    return jnp.concatenate(
        [
            jnp.broadcast_to(row[:, i : i + 128], (128, 128)).T
            for i in range(0, row.shape[1], 128)
        ],
        axis=0,
    )


def call(body, outs, name, flops, limit, scratch=(), **specs):
    return pl.pallas_call(
        body,
        **specs,
        out_shape=outs,
        scratch_shapes=list(scratch),
        name=name,
        compiler_params=pltpu.CompilerParams(vmem_limit_bytes=limit * MIB),
        cost_estimate=pl.CostEstimate(
            flops=flops, bytes_accessed=2 * MIB, transcendentals=0
        ),
    )


def shape(*dims, dtype=F32):
    return jax.ShapeDtypeStruct(dims, dtype)


def pack_kernel(emb_hbm, asg_hbm, out, emb, asg, sems):
    copies = [
        pltpu.make_async_copy(emb_hbm, emb, sems.at[0]),
        pltpu.make_async_copy(asg_hbm, asg, sems.at[1]),
    ]
    for c in copies:
        c.start()
    for c in copies:
        c.wait()
    xn = unit(emb[...].astype(F32)).astype(BF16)
    rows = []
    for it in range(2):
        a = asg[it : it + 1, :]
        owner = a >> 10
        own_f = owner.astype(F32)
        same = jnp.broadcast_to(own_f, (TOK, TOK)).T == own_f
        before = iota((TOK, TOK), 0) < iota((TOK, TOK), 1)
        rank = jnp.sum(jnp.where(same & before, 1.0, 0.0), axis=0, keepdims=True)
        code = (a & (KO - 1)) + 1
        rows.append((a >> 13, code >> 5, code & 31, (owner & 7) * 2 + rank.astype(jnp.int32)))
    zero = jnp.zeros((5, TOK), jnp.int32)
    for c in range(NC):
        out[c, 0:TOK, :] = xn
        parts = []
        for shard, hi, lo, place in rows:
            mine = shard == c
            parts += [jnp.where(mine, hi, 0), jnp.where(mine, lo, 0), place, zero]
        out[c, TOK : TOK + 16, :] = jnp.concatenate(parts, axis=0).astype(F32).astype(BF16)


def unpack_kernel(asg, rec, mass_out, res_out):
    masses = []
    for it in range(2):
        a = asg[it : it + 1, :]
        owner = a >> 10
        own_f = owner.astype(F32)
        same = jnp.broadcast_to(own_f, (TOK, TOK)).T == own_f
        before = iota((TOK, TOK), 0) < iota((TOK, TOK), 1)
        rank = jnp.sum(jnp.where(same & before, 1.0, 0.0), axis=0, keepdims=True)
        place = (owner.astype(F32) * 2.0 + rank) * 1.0
        shard = a >> 13
        row = shard.astype(F32) * 16.0 + (owner & 7).astype(F32) * 2.0 + rank
        col = column(row)
        lane = iota((TOK, 128), 1).astype(F32)
        oh = jnp.concatenate(
            [jnp.where(col == lane + 128.0 * j, 1.0, 0.0) for j in range(2)], axis=1
        ).astype(BF16)
        mrows = jnp.concatenate([rec[s, 16:32, :] for s in range(NC)], axis=0)
        m = mm(oh, mrows)
        masses.append(m.T[it : it + 1, :])
        if it == 1:
            rrows = jnp.concatenate([rec[s, 0:16, :] for s in range(NC)], axis=0)
            res_out[...] = mm(oh, rrows).astype(BF16)
    mass_out[...] = jnp.concatenate(masses, axis=0)


def cent_kernel(cent, out):
    @pl.loop(0, KC // 256)
    def _(i):
        at = pl.ds(pl.multiple_of(i * 256, 256), 256)
        out[at, :] = unit(cent[at, :].astype(F32)).astype(BF16)


def score_rows(rec, x):
    for s in range(NC):
        hi, lo = split(rec[s, 0:TOK, :].astype(F32) * SCALE)
        x[s * TOK : (s + 1) * TOK, :] = jnp.concatenate([hi, lo], axis=1)


def score_block(x, cblk, g, acc, shift, first):
    part = None
    for k in range(0, KO, KW):
        c = cblk[k : k + KW, :]
        e = mm(x[...], jnp.concatenate([c, c], axis=1), NT)
        if shift is not None:
            e = e + shift[:, k : k + KW]
        e = jnp.exp2(e)
        g[:, k : k + KW] = e.astype(BF16)
        for q in range(0, KW, 128):
            t = e[:, q : q + 128]
            part = t if part is None else part + t
    if first:
        acc[...] = part
    else:
        acc[...] += part


def finish_rows(acc, out):
    hi, lo = split(acc[...])
    one = jnp.ones((8, 128), BF16)
    r = mm(one, hi, NT) + mm(one, lo, NT)
    r = jnp.concatenate([r[0:1, s * 128 : (s + 1) * 128] for s in range(NC)], axis=0).astype(BF16)
    for c in range(NC):
        out[c] = r


def first_kernel(rec, cents, *refs):
    gs, (x, row_out, acc) = refs[:NO], refs[NO:]
    score_rows(rec, x)
    for o in range(NO):
        score_block(x, cents.at[o * KO : (o + 1) * KO], gs[o], acc, None, o == 0)
    finish_rows(acc, row_out)


def owner_onehot(idcol, o):
    ids = idcol[o * 32 : (o + 1) * 32, :]
    lane = iota((32, 128), 1).astype(F32)
    return jnp.concatenate(
        [jnp.where(ids == lane + (128.0 * j + 1.0), 1.0, 0.0) for j in range(KO // 128)],
        axis=1,
    ).astype(BF16)


def order_matrix(back):
    i, j = iota((SL, SL), 0), iota((SL, SL), 1)
    if back:
        want = ((i >> 1) & 7) * 32 + (i >> 4) * 2 + (i & 1)
    else:
        want = ((i >> 1) & 15) * 16 + (i >> 5) * 2 + (i & 1)
    return jnp.where(j == want, 1.0, 0.0).astype(BF16)


def slot_kernel(rec, cents, p_out, xs_out, id_out, col_out, cs_out):
    order = order_matrix(False)
    ids = []
    for it in range(2):
        base = TOK + 8 * it
        place16 = iota((16, TOK), 0).astype(F32)
        xs, digits = [], []
        for s in range(NC):
            meta = rec[s, base : base + 8, :].astype(F32)
            hi, lo, place = meta[0:1, :], meta[1:2, :], meta[2:3, :]
            p = jnp.where((place16 == place) & (hi + lo > 0.0), 1.0, 0.0)
            p_out[it, s * 16 : (s + 1) * 16, :] = p
            xs.append(mm(p.astype(BF16), rec[s, 0:TOK, :]))
            digits.append(
                jnp.concatenate(
                    [
                        jnp.broadcast_to(jnp.sum(p * q, axis=1, keepdims=True), (16, 128))
                        for q in (hi, lo)
                    ],
                    axis=1,
                )
            )
        both = jnp.concatenate([jnp.concatenate(xs, axis=0), jnp.concatenate(digits, axis=0)], axis=1)
        both = mm(order, both.astype(BF16))
        xs_out[it] = both[:, 0:128].astype(BF16)
        dhi, dlo = both[:, 128:256], both[:, 256:384]
        col = dhi * 32.0 + dlo
        col_out[it] = col
        rhi = jnp.concatenate([dhi[0:128].T[0:1], dhi[128:256].T[0:1]], axis=1)
        rlo = jnp.concatenate([dlo[0:128].T[0:1], dlo[128:256].T[0:1]], axis=1)
        at = (iota((SL, 128), 0) & 31) + 32 * it
        lane = jnp.where(iota((SL, 128), 1) == at, 1.0, 0.0).astype(BF16)
        own = iota((8, SL), 0) == (iota((8, SL), 1) >> 5)
        rows = jnp.concatenate([jnp.where(own, rhi, 0.0), jnp.where(own, rlo, 0.0)], axis=0)
        ids.append(mm(rows.astype(BF16), lane))
        if it == 0:
            for o in range(NO):
                cs_out[o * 32 : (o + 1) * 32, :] = mm(
                    owner_onehot(col, o), cents[o * KO : (o + 1) * KO, :]
                ).astype(BF16)
    id_out[...] = (ids[0] + ids[1]).astype(BF16)


def colsum_kernel(it, rowp, p_in, xs_in, cs_in, meta, *refs):
    gs, (out, w_out, ucol, tots) = refs[:NO], refs[NO:]
    u = 1.0 / jnp.sum(rowp[...].astype(F32), axis=0)
    for s in range(NC):
        ucol[s * 128 : (s + 1) * 128, :] = jnp.broadcast_to(u[s : s + 1, :], (128, 128)).T.astype(BF16)
    W = 512
    for o in range(NO):
        for h in range(KO // W):

            def body(j, acc):
                at = pl.ds(pl.multiple_of(j * 128, 128), 128)
                uu = ucol[at, :]
                prod = gs[o][at, h * W : (h + 1) * W] * jnp.concatenate([uu] * (W // 128), axis=1)
                prod = prod[0:64] + prod[64:128]
                prod = (prod[0:32] + prod[32:64]).astype(F32)
                return acc + ((prod[0:8] + prod[8:16]) + (prod[16:24] + prod[24:32]))

            acc = lax.fori_loop(0, T // 128, body, jnp.zeros((8, W), F32), unroll=8)
            tot = jnp.sum(acc, axis=0, keepdims=True)
            row = (o * KO + h * W) // 128
            for q in range(W // 128):
                tots[row + q : row + q + 1, :] = tot[:, q * 128 : (q + 1) * 128]
    us = jnp.concatenate(
        [
            jnp.sum(p_in[it, s * 16 : (s + 1) * 16, :] * u[s : s + 1, :], axis=1, keepdims=True)
            for s in range(NC)
        ],
        axis=0,
    )
    uhi, ulo = split(jnp.broadcast_to(us, (SL, 128)))
    both = mm(order_matrix(False), jnp.concatenate([uhi, ulo], axis=1))
    us = both[:, 0:128] + both[:, 128:256]
    xs = xs_in[it].astype(F32)
    aff = jnp.sum(xs * cs_in[...].astype(F32), axis=1, keepdims=True)
    w = (CENTROIDS * jnp.exp2(aff * SCALE)) * us
    w_out[...] = w
    rows = (w * xs).astype(BF16)
    if it == 0:
        tot = tots[...].astype(BF16)
    else:
        got = jnp.concatenate([slot_values(o, meta, tots)[1] for o in range(NO)], axis=0)
        tot = jnp.concatenate([got[:, 0:128], got[:, 128:256]], axis=0).astype(BF16)
    base = tot.shape[0]
    for d in range(ND):
        out[d, 0:base, :] = tot
        out[d, base : base + SL, :] = rows
        if it == 0:
            out[d, 320:336, :] = meta[...]


def slot_codes(rec, it):
    mine = (iota((16, 128), 1) >> 5) == it
    halves = []
    for h in range(2):
        tot = jnp.zeros((16, 128), F32)
        for q in range(4):
            ids = jnp.where(mine, rec[4 * h + q, 320:336, :].astype(F32), 0.0)
            by = 32 * ((q - it) % 4)
            tot = tot + (pltpu.roll(ids, by, 1) if by else ids)
        halves.append(tot)
    both = jnp.concatenate(halves, axis=1)
    return both[0:8] * 32.0 + both[8:16]


def own_row(values):
    at = lax.axis_index("dp") * 32 + (iota((SL, SL), 1) & 31)
    pick = jnp.where(iota((SL, SL), 0) == at, 1.0, 0.0).astype(BF16)
    hi, lo = split(values)
    got = mm(jnp.concatenate([hi, lo], axis=0), pick)
    got = got[0:8] + got[8:16]
    own = iota((8, SL), 0) == (iota((8, SL), 1) >> 5)
    return jnp.sum(jnp.where(own, got, 0.0), axis=0, keepdims=True)


def slot_values(o, codes, table):
    pos = (codes[o : o + 1, :] - 1.0).astype(jnp.int32)
    hi, lo = split(table[o * 8 : (o + 1) * 8, :])
    oh = jnp.where(iota((128, 256), 0) == (pos & 127), 1.0, 0.0).astype(BF16)
    got = mm(jnp.concatenate([hi, lo], axis=0), oh)
    got = got[0:8] + got[8:16]
    val = jnp.sum(jnp.where(iota((8, 256), 0) == (pos >> 7), got, 0.0), axis=0, keepdims=True)
    return pos, val


def slot_rows(o, rec, base):
    return jnp.concatenate(
        [rec[d, base + o * 32 : base + (o + 1) * 32, :] for d in range(ND)], axis=0
    )


def refine(o, pos, vs, rows, old, new):
    oht = jnp.where(iota((KO, 256), 0) == pos, vs, 0.0).astype(BF16)
    at = slice(o * KO, (o + 1) * KO)
    z = old[at, :].astype(F32) + mm(oht, rows)
    new[at, :] = unit(z).astype(BF16)


def second_kernel(rec, target, col_in, w_in, old, x, *refs):
    gs, (new_hbm, row_out, mass_out, cs_out, code_out, tv_out) = refs[:NO], refs[NO : 6 + NO]
    acc, vbuf, new, sem = refs[6 + NO :]
    tot = rec[0, 0:64, :].astype(F32)
    for d in range(1, ND):
        tot = tot + rec[d, 0:64, :].astype(F32)
    goal = target[...] * (TOKENS / CENTROIDS)
    v = goal / tot
    vbuf[...] = v
    logv = jnp.log2(v)
    codes = slot_codes(rec, 0)
    slots = [slot_values(o, codes, vbuf) for o in range(NO)]
    for o in range(NO):
        refine(o, *slots[o], slot_rows(o, rec, 64), old, new)
    save = pltpu.make_async_copy(new, new_hbm, sem)
    save.start()
    vs = jnp.concatenate([val for _, val in slots], axis=0)
    mass_out[...] = w_in[...] * column(own_row(vs))
    codes = slot_codes(rec, 1)
    code_out[...] = codes
    vbuf[...] = goal * v
    tv_out[...] = jnp.concatenate([slot_values(o, codes, vbuf)[1] for o in range(NO)], axis=0)
    col = col_in[1]
    for o in range(NO):
        cblk = new.at[o * KO : (o + 1) * KO]
        cs_out[o * 32 : (o + 1) * 32, :] = mm(owner_onehot(col, o), cblk[...]).astype(BF16)
        shift = jnp.concatenate([logv[o * 8 + q : o * 8 + q + 1, :] for q in range(8)], axis=1)
        score_block(x, cblk, gs[o], acc, shift, o == 0)
    finish_rows(acc, row_out)
    save.wait()


def last_potentials(rec, codes, tv):
    tot = rec[0, 0:16, :].astype(F32)
    for d in range(1, ND):
        tot = tot + rec[d, 0:16, :].astype(F32)
    tot = jnp.concatenate([tot[0:8], tot[8:16]], axis=1)
    some = codes[...] > 0.0
    return jnp.where(some, tv[...] / jnp.where(some, tot, 1.0), 0.0)


def tail_kernel(rec, codes, tv, col_in, xs_in, cs_in, w_in, mass1, out):
    vs = last_potentials(rec, codes, tv)
    mass2 = w_in[...] * column(own_row(vs))
    lane = iota((SL, 128), 1)
    m = jnp.where(lane == 0, mass1[...], jnp.where(lane == 1, mass2, 0.0))
    pos = (codes[...] - 1.0).astype(jnp.int32)
    col = col_in[1]
    new = []
    for o in range(NO):
        mine = col[o * 32 : (o + 1) * 32, :] - 1.0
        mine = jnp.concatenate([mine, mine], axis=1).astype(jnp.int32)
        oht = jnp.where(mine == pos[o : o + 1, :], vs[o : o + 1, :], 0.0).astype(BF16)
        z = cs_in[o * 32 : (o + 1) * 32, :].astype(F32) + mm(oht, slot_rows(o, rec, 16))
        new.append(unit(z).astype(BF16).astype(F32))
    r = xs_in[1].astype(F32) - jnp.concatenate(new, axis=0)
    both = jnp.concatenate([r.astype(BF16), m.astype(BF16)], axis=1)
    both = mm(order_matrix(True), both).astype(BF16)
    for s in range(NC):
        out[s, 0:16, :] = both[s * 16 : (s + 1) * 16, 0:128]
        out[s, 16:32, :] = both[s * 16 : (s + 1) * 16, 128:256]


def last_kernel(rec, codes, tv, old, new):
    vs = last_potentials(rec, codes, tv)
    pos = (codes[...] - 1.0).astype(jnp.int32)
    for o in range(NO):
        refine(o, pos[o : o + 1, :], vs[o : o + 1, :], slot_rows(o, rec, 16), old, new)


def exchange(x, axis):
    return lax.all_to_all(x, axis, 0, 0, tiled=True)


def on_device(embeddings, centroids, col_mass, assignments):
    target = col_mass.reshape(KC // 128, 128)
    gshape = tuple(pltpu.VMEM((T, KO), BF16) for _ in range(NO))
    sums = shape(NC, NC, 128, dtype=BF16)
    racc = (pltpu.VMEM((T, 128), F32),)
    pay = call(
        pack_kernel,
        shape(NC, TOK + 16, 128, dtype=BF16),
        "pack",
        10**6,
        8,
        (pltpu.VMEM((TOK, D), BF16), pltpu.VMEM((2, TOK), jnp.int32), pltpu.SemaphoreType.DMA((2,))),
        in_specs=[pl.BlockSpec(memory_space=pltpu.HBM)] * 2,
    )(*(pltpu.with_memory_space_constraint(a, pltpu.HBM) for a in (embeddings, assignments)))
    rec = exchange(pay, "cent")
    c0 = call(cent_kernel, shape(KC, D, dtype=BF16), "cents", 10**9, 12)(centroids)
    p, xs, ids, col, cs = call(
        slot_kernel,
        (
            shape(2, SL, TOK),
            shape(2, SL, D, dtype=BF16),
            shape(16, 128, dtype=BF16),
            shape(2, SL, 128),
            shape(SL, D, dtype=BF16),
        ),
        "slots",
        10**9,
        12,
    )(rec, c0)
    rec, c0, xs = lax.optimization_barrier((rec, c0, xs))

    def columns(it, rows, cs, meta, g):
        def body(*refs):
            colsum_kernel(it, *refs)

        out, w = call(
            body,
            (shape(ND, 272 if it else 336, 128, dtype=BF16), shape(SL, 128)),
            f"columns{it}",
            10**9,
            12,
            (pltpu.VMEM((T, 128), BF16), pltpu.VMEM((64, 128), F32)),
        )(rows, p, xs, cs, meta, *g)
        return exchange(out, "dp"), w

    *g, x, rows = call(
        first_kernel, gshape + (pltpu.VMEM((T, 2 * D), BF16), sums), "first", 10**10, 12, racc
    )(rec, c0)
    rows = exchange(rows, "cent")
    got, w = columns(0, rows, cs, ids, g)
    vmem = pl.BlockSpec(memory_space=pltpu.VMEM)
    *g, c1, rows, mass1, cs, codes, tv = call(
        second_kernel,
        gshape
        + (
            pltpu.HBM((KC, D), BF16),
            sums,
            shape(SL, 128),
            shape(SL, D, dtype=BF16),
            shape(NO, SL),
            shape(NO, SL),
        ),
        "second",
        10**10,
        12,
        racc + (pltpu.VMEM((KC // 128, 128), F32), pltpu.VMEM((KC, D), BF16), pltpu.SemaphoreType.DMA),
        out_specs=(vmem,) * NO + (pl.BlockSpec(memory_space=pltpu.HBM),) + (vmem,) * 5,
    )(got, target, col, w, c0, x)
    rows = exchange(rows, "cent")
    got, w = columns(1, rows, cs, codes, g)
    out = call(tail_kernel, shape(NC, 32, 128, dtype=BF16), "tail", 10**8, 12)(
        got, codes, tv, col, xs, cs, w, mass1
    )
    got, out = lax.optimization_barrier((got, out))
    back = exchange(out, "cent")
    c2 = call(last_kernel, shape(KC, D, dtype=BF16), "last", 10**9, 12)(got, codes, tv, c1)
    mass, res = call(unpack_kernel, (shape(2, TOK), shape(TOK, D, dtype=BF16)), "unpack", 10**6, 8)(
        assignments, back
    )
    return c2, mass, res


def solution(mesh):
    in_specs = (P(("dp", "cent"), None), P("cent", None), P("cent"), P(None, ("dp", "cent")))
    out_specs = (P("cent", None), P(None, ("dp", "cent")), P(("dp", "cent"), None))
    return jax.shard_map(
        on_device, mesh=mesh, in_specs=in_specs, out_specs=out_specs, check_vma=False
    )
```

```python
import math

import jax
import jax.numpy as jnp
from jax import lax
from jax.experimental import pallas as pl
from jax.experimental.pallas import tpu as pltpu
from jax.sharding import PartitionSpec as P

F32, BF16 = jnp.float32, jnp.bfloat16
D = 128
TOK = 128
NC, ND = 16, 8
T = TOK * NC
KC = 8192
NO, KO = 8, 1024
SL = 256
SCALE = 20.0 * math.log2(math.e)
TOKENS, CENTROIDS = 16384, 131072
KW = 256
MIB = 2**20

NN = (((1,), (0,)), ((), ()))
NT = (((1,), (1,)), ((), ()))


def mm(a, b, dims=NN):
    return lax.dot_general(a, b, dims, preferred_element_type=F32)


def iota(shape, dim):
    return lax.broadcasted_iota(jnp.int32, shape, dim)


def unit(z):
    return z * lax.rsqrt(jnp.sum(z * z, axis=1, keepdims=True) + 1e-06)


def split(z):
    hi = z.astype(BF16)
    return hi, (z - hi.astype(F32)).astype(BF16)


def column(row):
    return jnp.concatenate(
        [
            jnp.broadcast_to(row[:, i : i + 128], (128, 128)).T
            for i in range(0, row.shape[1], 128)
        ],
        axis=0,
    )


def call(body, outs, name, flops, limit, scratch=(), **specs):
    return pl.pallas_call(
        body,
        **specs,
        out_shape=outs,
        scratch_shapes=list(scratch),
        name=name,
        compiler_params=pltpu.CompilerParams(vmem_limit_bytes=limit * MIB),
        cost_estimate=pl.CostEstimate(
            flops=flops, bytes_accessed=2 * MIB, transcendentals=0
        ),
    )


def shape(*dims, dtype=F32):
    return jax.ShapeDtypeStruct(dims, dtype)


def pack_kernel(emb_hbm, asg_hbm, out, emb, asg, sems):
    copies = [
        pltpu.make_async_copy(emb_hbm, emb, sems.at[0]),
        pltpu.make_async_copy(asg_hbm, asg, sems.at[1]),
    ]
    for c in copies:
        c.start()
    for c in copies:
        c.wait()
    xn = unit(emb[...].astype(F32)).astype(BF16)
    rows = []
    for it in range(2):
        a = asg[it : it + 1, :]
        owner = a >> 10
        own_f = owner.astype(F32)
        same = jnp.broadcast_to(own_f, (TOK, TOK)).T == own_f
        before = iota((TOK, TOK), 0) < iota((TOK, TOK), 1)
        rank = jnp.sum(jnp.where(same & before, 1.0, 0.0), axis=0, keepdims=True)
        code = (a & (KO - 1)) + 1
        rows.append((a >> 13, code >> 5, code & 31, (owner & 7) * 2 + rank.astype(jnp.int32)))
    zero = jnp.zeros((5, TOK), jnp.int32)
    for c in range(NC):
        out[c, 0:TOK, :] = xn
        parts = []
        for shard, hi, lo, place in rows:
            mine = shard == c
            parts += [jnp.where(mine, hi, 0), jnp.where(mine, lo, 0), place, zero]
        out[c, TOK : TOK + 16, :] = jnp.concatenate(parts, axis=0).astype(F32).astype(BF16)


def unpack_kernel(asg, rec, mass_out, res_out):
    masses = []
    for it in range(2):
        a = asg[it : it + 1, :]
        owner = a >> 10
        own_f = owner.astype(F32)
        same = jnp.broadcast_to(own_f, (TOK, TOK)).T == own_f
        before = iota((TOK, TOK), 0) < iota((TOK, TOK), 1)
        rank = jnp.sum(jnp.where(same & before, 1.0, 0.0), axis=0, keepdims=True)
        place = (owner.astype(F32) * 2.0 + rank) * 1.0
        shard = a >> 13
        row = shard.astype(F32) * 16.0 + (owner & 7).astype(F32) * 2.0 + rank
        col = column(row)
        lane = iota((TOK, 128), 1).astype(F32)
        oh = jnp.concatenate(
            [jnp.where(col == lane + 128.0 * j, 1.0, 0.0) for j in range(2)], axis=1
        ).astype(BF16)
        mrows = jnp.concatenate([rec[s, 16:32, :] for s in range(NC)], axis=0)
        m = mm(oh, mrows)
        masses.append(m.T[it : it + 1, :])
        if it == 1:
            rrows = jnp.concatenate([rec[s, 0:16, :] for s in range(NC)], axis=0)
            res_out[...] = mm(oh, rrows).astype(BF16)
    mass_out[...] = jnp.concatenate(masses, axis=0)


def cent_kernel(cent, out):
    @pl.loop(0, KC // 256)
    def _(i):
        at = pl.ds(pl.multiple_of(i * 256, 256), 256)
        out[at, :] = unit(cent[at, :].astype(F32)).astype(BF16)


def score_rows(rec, x):
    for s in range(NC):
        hi, lo = split(rec[s, 0:TOK, :].astype(F32) * SCALE)
        x[s * TOK : (s + 1) * TOK, :] = jnp.concatenate([hi, lo], axis=1)


def score_block(x, cblk, g, acc, shift, first):
    part = None
    for k in range(0, KO, KW):
        c = cblk[k : k + KW, :]
        e = mm(x[...], jnp.concatenate([c, c], axis=1), NT)
        if shift is not None:
            e = e + shift[:, k : k + KW]
        e = jnp.exp2(e)
        g[:, k : k + KW] = e.astype(BF16)
        for q in range(0, KW, 128):
            t = e[:, q : q + 128]
            part = t if part is None else part + t
    if first:
        acc[...] = part
    else:
        acc[...] += part


def finish_rows(acc, out):
    hi, lo = split(acc[...])
    one = jnp.ones((8, 128), BF16)
    r = mm(one, hi, NT) + mm(one, lo, NT)
    r = jnp.concatenate([r[0:1, s * 128 : (s + 1) * 128] for s in range(NC)], axis=0).astype(BF16)
    for c in range(NC):
        out[c] = r


def owner_onehot(idcol, o):
    ids = idcol[o * 32 : (o + 1) * 32, :]
    lane = iota((32, 128), 1).astype(F32)
    return jnp.concatenate(
        [jnp.where(ids == lane + (128.0 * j + 1.0), 1.0, 0.0) for j in range(KO // 128)],
        axis=1,
    ).astype(BF16)


def order_matrix(back):
    i, j = iota((SL, SL), 0), iota((SL, SL), 1)
    if back:
        want = ((i >> 1) & 7) * 32 + (i >> 4) * 2 + (i & 1)
    else:
        want = ((i >> 1) & 15) * 16 + (i >> 5) * 2 + (i & 1)
    return jnp.where(j == want, 1.0, 0.0).astype(BF16)


def affinity(xs, cs):
    dot = jnp.sum(xs * cs, axis=1, keepdims=True)
    return jnp.broadcast_to(CENTROIDS * jnp.exp2(dot * SCALE), (SL, 128))


def slot_lists(rec, cents, p_out, xs_out, id_out, col_out, aff_out):
    order = order_matrix(False)
    ids = []
    for it in range(2):
        base = TOK + 8 * it
        place16 = iota((16, TOK), 0).astype(F32)
        xs, digits = [], []
        for s in range(NC):
            meta = rec[s, base : base + 8, :].astype(F32)
            hi, lo, place = meta[0:1, :], meta[1:2, :], meta[2:3, :]
            p = jnp.where((place16 == place) & (hi + lo > 0.0), 1.0, 0.0)
            p_out[it, s * 16 : (s + 1) * 16, :] = p
            xs.append(mm(p.astype(BF16), rec[s, 0:TOK, :]))
            digits.append(
                jnp.concatenate(
                    [
                        jnp.broadcast_to(jnp.sum(p * q, axis=1, keepdims=True), (16, 128))
                        for q in (hi, lo)
                    ],
                    axis=1,
                )
            )
        both = jnp.concatenate([jnp.concatenate(xs, axis=0), jnp.concatenate(digits, axis=0)], axis=1)
        both = mm(order, both.astype(BF16))
        xs_out[it] = both[:, 0:128].astype(BF16)
        dhi, dlo = both[:, 128:256], both[:, 256:384]
        col = dhi * 32.0 + dlo
        col_out[it] = col
        rhi = jnp.concatenate([dhi[0:128].T[0:1], dhi[128:256].T[0:1]], axis=1)
        rlo = jnp.concatenate([dlo[0:128].T[0:1], dlo[128:256].T[0:1]], axis=1)
        at = (iota((SL, 128), 0) & 31) + 32 * it
        lane = jnp.where(iota((SL, 128), 1) == at, 1.0, 0.0).astype(BF16)
        own = iota((8, SL), 0) == (iota((8, SL), 1) >> 5)
        rows = jnp.concatenate([jnp.where(own, rhi, 0.0), jnp.where(own, rlo, 0.0)], axis=0)
        ids.append(mm(rows.astype(BF16), lane))
        if it == 0:
            cs = [
                mm(owner_onehot(col, o), cents[o * KO : (o + 1) * KO, :]) for o in range(NO)
            ]
            aff_out[...] = affinity(both[:, 0:128], jnp.concatenate(cs, axis=0))
    id_out[...] = (ids[0] + ids[1]).astype(BF16)


def first_kernel(rec, cents, *refs):
    gs, (x, row_out), slot_refs, acc = refs[:NO], refs[NO : NO + 2], refs[NO + 2 : -1], refs[-1]
    score_rows(rec, x)
    for o in range(NO):
        score_block(x, cents.at[o * KO : (o + 1) * KO], gs[o], acc, None, o == 0)
        if o == 0:
            slot_lists(rec, cents, *slot_refs)
    finish_rows(acc, row_out)


def colsum_kernel(it, rowp, p_in, xs_in, aff_in, meta, *refs):
    gs, (out, w_out, ucol, tots) = refs[:NO], refs[NO:]
    u = 1.0 / jnp.sum(rowp[...].astype(F32), axis=0)
    for s in range(NC):
        ucol[s * 128 : (s + 1) * 128, :] = jnp.broadcast_to(u[s : s + 1, :], (128, 128)).T.astype(BF16)
    W = 512
    for o in range(NO):
        for h in range(KO // W):

            def body(j, acc):
                at = pl.ds(pl.multiple_of(j * 128, 128), 128)
                uu = ucol[at, :]
                prod = gs[o][at, h * W : (h + 1) * W] * jnp.concatenate([uu] * (W // 128), axis=1)
                prod = prod[0:64] + prod[64:128]
                prod = (prod[0:32] + prod[32:64]).astype(F32)
                return acc + ((prod[0:8] + prod[8:16]) + (prod[16:24] + prod[24:32]))

            acc = lax.fori_loop(0, T // 128, body, jnp.zeros((8, W), F32), unroll=8)
            tot = jnp.sum(acc, axis=0, keepdims=True)
            row = (o * KO + h * W) // 128
            for q in range(W // 128):
                tots[row + q : row + q + 1, :] = tot[:, q * 128 : (q + 1) * 128]
    us = jnp.concatenate(
        [
            jnp.sum(p_in[it, s * 16 : (s + 1) * 16, :] * u[s : s + 1, :], axis=1, keepdims=True)
            for s in range(NC)
        ],
        axis=0,
    )
    uhi, ulo = split(jnp.broadcast_to(us, (SL, 128)))
    both = mm(order_matrix(False), jnp.concatenate([uhi, ulo], axis=1))
    us = both[:, 0:128] + both[:, 128:256]
    w = aff_in[...] * us
    w_out[...] = w
    rows = (w * xs_in[it].astype(F32)).astype(BF16)
    if it == 0:
        tot = tots[...].astype(BF16)
    else:
        got = jnp.concatenate([slot_values(o, meta, tots)[1] for o in range(NO)], axis=0)
        tot = jnp.concatenate([got[:, 0:128], got[:, 128:256]], axis=0).astype(BF16)
    base = tot.shape[0]
    for d in range(ND):
        out[d, 0:base, :] = tot
        out[d, base : base + SL, :] = rows
        if it == 0:
            out[d, 320:336, :] = meta[...]


def slot_codes(rec, it):
    mine = (iota((16, 128), 1) >> 5) == it
    halves = []
    for h in range(2):
        tot = jnp.zeros((16, 128), F32)
        for q in range(4):
            ids = jnp.where(mine, rec[4 * h + q, 320:336, :].astype(F32), 0.0)
            by = 32 * ((q - it) % 4)
            tot = tot + (pltpu.roll(ids, by, 1) if by else ids)
        halves.append(tot)
    both = jnp.concatenate(halves, axis=1)
    return both[0:8] * 32.0 + both[8:16]


def own_row(values):
    at = lax.axis_index("dp") * 32 + (iota((SL, SL), 1) & 31)
    pick = jnp.where(iota((SL, SL), 0) == at, 1.0, 0.0).astype(BF16)
    hi, lo = split(values)
    got = mm(jnp.concatenate([hi, lo], axis=0), pick)
    got = got[0:8] + got[8:16]
    own = iota((8, SL), 0) == (iota((8, SL), 1) >> 5)
    return jnp.sum(jnp.where(own, got, 0.0), axis=0, keepdims=True)


def slot_values(o, codes, table):
    pos = (codes[o : o + 1, :] - 1.0).astype(jnp.int32)
    hi, lo = split(table[o * 8 : (o + 1) * 8, :])
    oh = jnp.where(iota((128, 256), 0) == (pos & 127), 1.0, 0.0).astype(BF16)
    got = mm(jnp.concatenate([hi, lo], axis=0), oh)
    got = got[0:8] + got[8:16]
    val = jnp.sum(jnp.where(iota((8, 256), 0) == (pos >> 7), got, 0.0), axis=0, keepdims=True)
    return pos, val


def slot_rows(o, rec, base):
    return jnp.concatenate(
        [rec[d, base + o * 32 : base + (o + 1) * 32, :] for d in range(ND)], axis=0
    )


def refine(o, pos, vs, rows, old, new):
    oht = jnp.where(iota((KO, 256), 0) == pos, vs, 0.0).astype(BF16)
    at = slice(o * KO, (o + 1) * KO)
    z = old[at, :].astype(F32) + mm(oht, rows)
    new[at, :] = unit(z).astype(BF16)


def second_kernel(rec, target, col_in, xs_in, w_in, old, x, *refs):
    gs, (new_hbm, row_out, mass_out, cs_out, aff_out, code_out, tv_out) = refs[:NO], refs[NO : 7 + NO]
    acc, vbuf, new, sem = refs[7 + NO :]
    tot = rec[0, 0:64, :].astype(F32)
    for d in range(1, ND):
        tot = tot + rec[d, 0:64, :].astype(F32)
    goal = target[...] * (TOKENS / CENTROIDS)
    v = goal / tot
    vbuf[...] = v
    logv = jnp.log2(v)
    codes = slot_codes(rec, 0)
    slots = [slot_values(o, codes, vbuf) for o in range(NO)]
    for o in range(NO):
        refine(o, *slots[o], slot_rows(o, rec, 64), old, new)
    save = pltpu.make_async_copy(new, new_hbm, sem)
    save.start()
    vs = jnp.concatenate([val for _, val in slots], axis=0)
    mass_out[...] = w_in[...] * column(own_row(vs))
    codes = slot_codes(rec, 1)
    code_out[...] = codes
    vbuf[...] = goal * v
    tv_out[...] = jnp.concatenate([slot_values(o, codes, vbuf)[1] for o in range(NO)], axis=0)
    col = col_in[1]
    for o in range(NO):
        cblk = new.at[o * KO : (o + 1) * KO]
        cs_out[o * 32 : (o + 1) * 32, :] = mm(owner_onehot(col, o), cblk[...]).astype(BF16)
        shift = jnp.concatenate([logv[o * 8 + q : o * 8 + q + 1, :] for q in range(8)], axis=1)
        score_block(x, cblk, gs[o], acc, shift, o == 0)
    aff_out[...] = affinity(xs_in[1].astype(F32), cs_out[...].astype(F32))
    finish_rows(acc, row_out)
    save.wait()


def last_potentials(rec, codes, tv):
    tot = rec[0, 0:16, :].astype(F32)
    for d in range(1, ND):
        tot = tot + rec[d, 0:16, :].astype(F32)
    tot = jnp.concatenate([tot[0:8], tot[8:16]], axis=1)
    some = codes[...] > 0.0
    return jnp.where(some, tv[...] / jnp.where(some, tot, 1.0), 0.0)


def tail_kernel(rec, codes, tv, col_in, xs_in, cs_in, w_in, mass1, out):
    vs = last_potentials(rec, codes, tv)
    mass2 = w_in[...] * column(own_row(vs))
    lane = iota((SL, 128), 1)
    m = jnp.where(lane == 0, mass1[...], jnp.where(lane == 1, mass2, 0.0))
    pos = (codes[...] - 1.0).astype(jnp.int32)
    col = col_in[1]
    new = []
    for o in range(NO):
        mine = col[o * 32 : (o + 1) * 32, :] - 1.0
        mine = jnp.concatenate([mine, mine], axis=1).astype(jnp.int32)
        oht = jnp.where(mine == pos[o : o + 1, :], vs[o : o + 1, :], 0.0).astype(BF16)
        z = cs_in[o * 32 : (o + 1) * 32, :].astype(F32) + mm(oht, slot_rows(o, rec, 16))
        new.append(unit(z).astype(BF16).astype(F32))
    r = xs_in[1].astype(F32) - jnp.concatenate(new, axis=0)
    both = jnp.concatenate([r.astype(BF16), m.astype(BF16)], axis=1)
    both = mm(order_matrix(True), both).astype(BF16)
    for s in range(NC):
        out[s, 0:16, :] = both[s * 16 : (s + 1) * 16, 0:128]
        out[s, 16:32, :] = both[s * 16 : (s + 1) * 16, 128:256]


def last_kernel(rec, codes, tv, old, new):
    vs = last_potentials(rec, codes, tv)
    pos = (codes[...] - 1.0).astype(jnp.int32)
    for o in range(NO):
        refine(o, pos[o : o + 1, :], vs[o : o + 1, :], slot_rows(o, rec, 16), old, new)


def exchange(x, axis):
    return lax.all_to_all(x, axis, 0, 0, tiled=True)


def on_device(embeddings, centroids, col_mass, assignments):
    target = col_mass.reshape(KC // 128, 128)
    gshape = tuple(pltpu.VMEM((T, KO), BF16) for _ in range(NO))
    sums = shape(NC, NC, 128, dtype=BF16)
    racc = (pltpu.VMEM((T, 128), F32),)
    pay = call(
        pack_kernel,
        shape(NC, TOK + 16, 128, dtype=BF16),
        "pack",
        10**6,
        8,
        (pltpu.VMEM((TOK, D), BF16), pltpu.VMEM((2, TOK), jnp.int32), pltpu.SemaphoreType.DMA((2,))),
        in_specs=[pl.BlockSpec(memory_space=pltpu.HBM)] * 2,
    )(*(pltpu.with_memory_space_constraint(a, pltpu.HBM) for a in (embeddings, assignments)))
    rec = exchange(pay, "cent")
    c0 = call(cent_kernel, shape(KC, D, dtype=BF16), "cents", 10**9, 12)(centroids)
    *g, x, rows, p, xs, ids, col, aff = call(
        first_kernel,
        gshape
        + (
            pltpu.VMEM((T, 2 * D), BF16),
            sums,
            shape(2, SL, TOK),
            shape(2, SL, D, dtype=BF16),
            shape(16, 128, dtype=BF16),
            shape(2, SL, 128),
            shape(SL, 128),
        ),
        "first",
        10**10,
        14,
        racc,
    )(rec, c0)
    rows = exchange(rows, "cent")

    def columns(it, rows, aff, meta, g):
        def body(*refs):
            colsum_kernel(it, *refs)

        out, w = call(
            body,
            (shape(ND, 272 if it else 336, 128, dtype=BF16), shape(SL, 128)),
            f"columns{it}",
            10**9,
            12,
            (pltpu.VMEM((T, 128), BF16), pltpu.VMEM((64, 128), F32)),
        )(rows, p, xs, aff, meta, *g)
        return exchange(out, "dp"), w

    got, w = columns(0, rows, aff, ids, g)
    vmem = pl.BlockSpec(memory_space=pltpu.VMEM)
    *g, c1, rows, mass1, cs, aff, codes, tv = call(
        second_kernel,
        gshape
        + (
            pltpu.HBM((KC, D), BF16),
            sums,
            shape(SL, 128),
            shape(SL, D, dtype=BF16),
            shape(SL, 128),
            shape(NO, SL),
            shape(NO, SL),
        ),
        "second",
        10**10,
        12,
        racc + (pltpu.VMEM((KC // 128, 128), F32), pltpu.VMEM((KC, D), BF16), pltpu.SemaphoreType.DMA),
        out_specs=(vmem,) * NO + (pl.BlockSpec(memory_space=pltpu.HBM),) + (vmem,) * 6,
    )(got, target, col, xs, w, c0, x)
    rows = exchange(rows, "cent")
    got, w = columns(1, rows, aff, codes, g)
    out = call(tail_kernel, shape(NC, 32, 128, dtype=BF16), "tail", 10**8, 12)(
        got, codes, tv, col, xs, cs, w, mass1
    )
    got, out = lax.optimization_barrier((got, out))
    back = exchange(out, "cent")
    c2 = call(last_kernel, shape(KC, D, dtype=BF16), "last", 10**9, 12)(got, codes, tv, c1)
    mass, res = call(unpack_kernel, (shape(2, TOK), shape(TOK, D, dtype=BF16)), "unpack", 10**6, 8)(
        assignments, back
    )
    return c2, mass, res


def solution(mesh):
    in_specs = (P(("dp", "cent"), None), P("cent", None), P("cent"), P(None, ("dp", "cent")))
    out_specs = (P("cent", None), P(None, ("dp", "cent")), P(("dp", "cent"), None))
    return jax.shard_map(
        on_device, mesh=mesh, in_specs=in_specs, out_specs=out_specs, check_vma=False
    )
```

```python
import math

import jax
import jax.numpy as jnp
from jax import lax
from jax.experimental import pallas as pl
from jax.experimental.pallas import tpu as pltpu
from jax.sharding import PartitionSpec as P

F32, BF16 = jnp.float32, jnp.bfloat16
D = 128
TOK = 128
NC, ND = 16, 8
T = TOK * NC
KC = 8192
NO, KO = 8, 1024
SL = 256
SCALE = 20.0 * math.log2(math.e)
TOKENS, CENTROIDS = 16384, 131072
TR = 256
MIB = 2**20

NN = (((1,), (0,)), ((), ()))
NT = (((1,), (1,)), ((), ()))


def mm(a, b, dims=NN):
    return lax.dot_general(a, b, dims, preferred_element_type=F32)


def iota(shape, dim):
    return lax.broadcasted_iota(jnp.int32, shape, dim)


def unit(z):
    return z * lax.rsqrt(jnp.sum(z * z, axis=1, keepdims=True) + 1e-06)


def split(z):
    hi = z.astype(BF16)
    return hi, (z - hi.astype(F32)).astype(BF16)


def column(row):
    return jnp.concatenate(
        [
            jnp.broadcast_to(row[:, i : i + 128], (128, 128)).T
            for i in range(0, row.shape[1], 128)
        ],
        axis=0,
    )


def call(body, outs, name, flops, limit, scratch=(), **specs):
    return pl.pallas_call(
        body,
        **specs,
        out_shape=outs,
        scratch_shapes=list(scratch),
        name=name,
        compiler_params=pltpu.CompilerParams(vmem_limit_bytes=limit * MIB),
        cost_estimate=pl.CostEstimate(
            flops=flops, bytes_accessed=2 * MIB, transcendentals=0
        ),
    )


def shape(*dims, dtype=F32):
    return jax.ShapeDtypeStruct(dims, dtype)


def pack_kernel(emb_hbm, asg_hbm, out, emb, asg, sems):
    copies = [
        pltpu.make_async_copy(emb_hbm, emb, sems.at[0]),
        pltpu.make_async_copy(asg_hbm, asg, sems.at[1]),
    ]
    for c in copies:
        c.start()
    for c in copies:
        c.wait()
    xn = unit(emb[...].astype(F32)).astype(BF16)
    rows = []
    for it in range(2):
        a = asg[it : it + 1, :]
        owner = a >> 10
        own_f = owner.astype(F32)
        same = jnp.broadcast_to(own_f, (TOK, TOK)).T == own_f
        before = iota((TOK, TOK), 0) < iota((TOK, TOK), 1)
        rank = jnp.sum(jnp.where(same & before, 1.0, 0.0), axis=0, keepdims=True)
        code = (a & (KO - 1)) + 1
        rows.append((a >> 13, code >> 5, code & 31, (owner & 7) * 2 + rank.astype(jnp.int32)))
    zero = jnp.zeros((5, TOK), jnp.int32)
    for c in range(NC):
        out[c, 0:TOK, :] = xn
        parts = []
        for shard, hi, lo, place in rows:
            mine = shard == c
            parts += [jnp.where(mine, hi, 0), jnp.where(mine, lo, 0), place, zero]
        out[c, TOK : TOK + 16, :] = jnp.concatenate(parts, axis=0).astype(F32).astype(BF16)


def unpack_kernel(asg, rec, mass_out, res_out):
    masses = []
    for it in range(2):
        a = asg[it : it + 1, :]
        owner = a >> 10
        own_f = owner.astype(F32)
        same = jnp.broadcast_to(own_f, (TOK, TOK)).T == own_f
        before = iota((TOK, TOK), 0) < iota((TOK, TOK), 1)
        rank = jnp.sum(jnp.where(same & before, 1.0, 0.0), axis=0, keepdims=True)
        place = (owner.astype(F32) * 2.0 + rank) * 1.0
        shard = a >> 13
        row = shard.astype(F32) * 16.0 + (owner & 7).astype(F32) * 2.0 + rank
        col = column(row)
        lane = iota((TOK, 128), 1).astype(F32)
        oh = jnp.concatenate(
            [jnp.where(col == lane + 128.0 * j, 1.0, 0.0) for j in range(2)], axis=1
        ).astype(BF16)
        mrows = jnp.concatenate([rec[s, 16:32, :] for s in range(NC)], axis=0)
        m = mm(oh, mrows)
        masses.append(m.T[it : it + 1, :])
        if it == 1:
            rrows = jnp.concatenate([rec[s, 0:16, :] for s in range(NC)], axis=0)
            res_out[...] = mm(oh, rrows).astype(BF16)
    mass_out[...] = jnp.concatenate(masses, axis=0)


def cent_kernel(cent, out):
    @pl.loop(0, KC // 256)
    def _(i):
        at = pl.ds(pl.multiple_of(i * 256, 256), 256)
        out[at, :] = unit(cent[at, :].astype(F32)).astype(BF16)


def score_rows(rec, x):
    for s in range(NC):
        hi, lo = split(rec[s, 0:TOK, :].astype(F32) * SCALE)
        x[s * TOK : (s + 1) * TOK, :] = jnp.concatenate([hi, lo], axis=1)


def score_block(x, cblk, g, acc, shift, first):
    c = jnp.concatenate([cblk[...], cblk[...]], axis=1)
    for r in range(0, T, TR):
        at = slice(r, r + TR)
        e = mm(x[at, :], c, NT)
        if shift is not None:
            e = e + shift
        e = jnp.exp2(e)
        g[at, :] = e.astype(BF16)
        part = e[:, 0:128]
        for q in range(128, KO, 128):
            part = part + e[:, q : q + 128]
        if first:
            acc[at, :] = part
        else:
            acc[at, :] += part


def finish_rows(acc, out):
    hi, lo = split(acc[...])
    one = jnp.ones((8, 128), BF16)
    r = mm(one, hi, NT) + mm(one, lo, NT)
    r = jnp.concatenate([r[0:1, s * 128 : (s + 1) * 128] for s in range(NC)], axis=0).astype(BF16)
    for c in range(NC):
        out[c] = r


def first_kernel(rec, cents, *refs):
    gs, (x, row_out, acc) = refs[:NO], refs[NO:]
    score_rows(rec, x)
    for o in range(NO):
        score_block(x, cents.at[o * KO : (o + 1) * KO], gs[o], acc, None, o == 0)
    finish_rows(acc, row_out)


def owner_onehot(idcol, o):
    ids = idcol[o * 32 : (o + 1) * 32, :]
    lane = iota((32, 128), 1).astype(F32)
    return jnp.concatenate(
        [jnp.where(ids == lane + (128.0 * j + 1.0), 1.0, 0.0) for j in range(KO // 128)],
        axis=1,
    ).astype(BF16)


def order_matrix(back):
    i, j = iota((SL, SL), 0), iota((SL, SL), 1)
    if back:
        want = ((i >> 1) & 7) * 32 + (i >> 4) * 2 + (i & 1)
    else:
        want = ((i >> 1) & 15) * 16 + (i >> 5) * 2 + (i & 1)
    return jnp.where(j == want, 1.0, 0.0).astype(BF16)


def slot_kernel(rec, cents, p_out, xs_out, id_out, col_out, cs_out):
    order = order_matrix(False)
    ids = []
    for it in range(2):
        base = TOK + 8 * it
        place16 = iota((16, TOK), 0).astype(F32)
        xs, digits = [], []
        for s in range(NC):
            meta = rec[s, base : base + 8, :].astype(F32)
            hi, lo, place = meta[0:1, :], meta[1:2, :], meta[2:3, :]
            p = jnp.where((place16 == place) & (hi + lo > 0.0), 1.0, 0.0)
            p_out[it, s * 16 : (s + 1) * 16, :] = p
            xs.append(mm(p.astype(BF16), rec[s, 0:TOK, :]))
            digits.append(
                jnp.concatenate(
                    [
                        jnp.broadcast_to(jnp.sum(p * q, axis=1, keepdims=True), (16, 128))
                        for q in (hi, lo)
                    ],
                    axis=1,
                )
            )
        both = jnp.concatenate([jnp.concatenate(xs, axis=0), jnp.concatenate(digits, axis=0)], axis=1)
        both = mm(order, both.astype(BF16))
        xs_out[it] = both[:, 0:128].astype(BF16)
        dhi, dlo = both[:, 128:256], both[:, 256:384]
        col = dhi * 32.0 + dlo
        col_out[it] = col
        rhi = jnp.concatenate([dhi[0:128].T[0:1], dhi[128:256].T[0:1]], axis=1)
        rlo = jnp.concatenate([dlo[0:128].T[0:1], dlo[128:256].T[0:1]], axis=1)
        at = (iota((SL, 128), 0) & 31) + 32 * it
        lane = jnp.where(iota((SL, 128), 1) == at, 1.0, 0.0).astype(BF16)
        own = iota((8, SL), 0) == (iota((8, SL), 1) >> 5)
        rows = jnp.concatenate([jnp.where(own, rhi, 0.0), jnp.where(own, rlo, 0.0)], axis=0)
        ids.append(mm(rows.astype(BF16), lane))
        if it == 0:
            for o in range(NO):
                cs_out[o * 32 : (o + 1) * 32, :] = mm(
                    owner_onehot(col, o), cents[o * KO : (o + 1) * KO, :]
                ).astype(BF16)
    id_out[...] = (ids[0] + ids[1]).astype(BF16)


def colsum_kernel(it, rowp, p_in, xs_in, cs_in, meta, *refs):
    gs, (out, w_out, ucol, tots) = refs[:NO], refs[NO:]
    u = 1.0 / jnp.sum(rowp[...].astype(F32), axis=0)
    for s in range(NC):
        ucol[s * 128 : (s + 1) * 128, :] = jnp.broadcast_to(u[s : s + 1, :], (128, 128)).T.astype(BF16)
    W = 512
    for o in range(NO):
        for h in range(KO // W):

            def body(j, acc):
                at = pl.ds(pl.multiple_of(j * 128, 128), 128)
                uu = ucol[at, :]
                prod = gs[o][at, h * W : (h + 1) * W] * jnp.concatenate([uu] * (W // 128), axis=1)
                prod = prod[0:64] + prod[64:128]
                prod = prod[0:32] + prod[32:64]
                prod = (prod[0:16] + prod[16:32]).astype(F32)
                return acc + (prod[0:8] + prod[8:16])

            acc = lax.fori_loop(0, T // 128, body, jnp.zeros((8, W), F32), unroll=8)
            tot = jnp.sum(acc, axis=0, keepdims=True)
            row = (o * KO + h * W) // 128
            for q in range(W // 128):
                tots[row + q : row + q + 1, :] = tot[:, q * 128 : (q + 1) * 128]
    us = jnp.concatenate(
        [
            jnp.sum(p_in[it, s * 16 : (s + 1) * 16, :] * u[s : s + 1, :], axis=1, keepdims=True)
            for s in range(NC)
        ],
        axis=0,
    )
    uhi, ulo = split(jnp.broadcast_to(us, (SL, 128)))
    both = mm(order_matrix(False), jnp.concatenate([uhi, ulo], axis=1))
    us = both[:, 0:128] + both[:, 128:256]
    xs = xs_in[it].astype(F32)
    aff = jnp.sum(xs * cs_in[...].astype(F32), axis=1, keepdims=True)
    w = (CENTROIDS * jnp.exp2(aff * SCALE)) * us
    w_out[...] = w
    rows = (w * xs).astype(BF16)
    if it == 0:
        tot = tots[...].astype(BF16)
    else:
        got = jnp.concatenate([slot_values(o, meta, tots)[1] for o in range(NO)], axis=0)
        tot = jnp.concatenate([got[:, 0:128], got[:, 128:256]], axis=0).astype(BF16)
    base = tot.shape[0]
    for d in range(ND):
        out[d, 0:base, :] = tot
        out[d, base : base + SL, :] = rows
        if it == 0:
            out[d, 320:336, :] = meta[...]


def slot_codes(rec, it):
    mine = (iota((16, 128), 1) >> 5) == it
    halves = []
    for h in range(2):
        tot = jnp.zeros((16, 128), F32)
        for q in range(4):
            ids = jnp.where(mine, rec[4 * h + q, 320:336, :].astype(F32), 0.0)
            by = 32 * ((q - it) % 4)
            tot = tot + (pltpu.roll(ids, by, 1) if by else ids)
        halves.append(tot)
    both = jnp.concatenate(halves, axis=1)
    return both[0:8] * 32.0 + both[8:16]


def own_row(values):
    at = lax.axis_index("dp") * 32 + (iota((SL, SL), 1) & 31)
    pick = jnp.where(iota((SL, SL), 0) == at, 1.0, 0.0).astype(BF16)
    hi, lo = split(values)
    got = mm(jnp.concatenate([hi, lo], axis=0), pick)
    got = got[0:8] + got[8:16]
    own = iota((8, SL), 0) == (iota((8, SL), 1) >> 5)
    return jnp.sum(jnp.where(own, got, 0.0), axis=0, keepdims=True)


def slot_values(o, codes, table):
    pos = (codes[o : o + 1, :] - 1.0).astype(jnp.int32)
    hi, lo = split(table[o * 8 : (o + 1) * 8, :])
    oh = jnp.where(iota((128, 256), 0) == (pos & 127), 1.0, 0.0).astype(BF16)
    got = mm(jnp.concatenate([hi, lo], axis=0), oh)
    got = got[0:8] + got[8:16]
    val = jnp.sum(jnp.where(iota((8, 256), 0) == (pos >> 7), got, 0.0), axis=0, keepdims=True)
    return pos, val


def slot_rows(o, rec, base):
    return jnp.concatenate(
        [rec[d, base + o * 32 : base + (o + 1) * 32, :] for d in range(ND)], axis=0
    )


def refine(o, pos, vs, rows, old, new):
    oht = jnp.where(iota((KO, 256), 0) == pos, vs, 0.0).astype(BF16)
    at = slice(o * KO, (o + 1) * KO)
    z = old[at, :].astype(F32) + mm(oht, rows)
    new[at, :] = unit(z).astype(BF16)


def second_kernel(rec, target, col_in, w_in, old, x, *refs):
    gs, (new_hbm, row_out, mass_out, cs_out, code_out, tv_out) = refs[:NO], refs[NO : 6 + NO]
    acc, vbuf, new, sem = refs[6 + NO :]
    tot = rec[0, 0:64, :].astype(F32)
    for d in range(1, ND):
        tot = tot + rec[d, 0:64, :].astype(F32)
    goal = target[...] * (TOKENS / CENTROIDS)
    v = goal / tot
    vbuf[...] = v
    logv = jnp.log2(v)
    codes = slot_codes(rec, 0)
    slots = [slot_values(o, codes, vbuf) for o in range(NO)]
    for o in range(NO):
        refine(o, *slots[o], slot_rows(o, rec, 64), old, new)
    save = pltpu.make_async_copy(new, new_hbm, sem)
    save.start()
    vs = jnp.concatenate([val for _, val in slots], axis=0)
    mass_out[...] = w_in[...] * column(own_row(vs))
    codes = slot_codes(rec, 1)
    code_out[...] = codes
    vbuf[...] = goal * v
    tv_out[...] = jnp.concatenate([slot_values(o, codes, vbuf)[1] for o in range(NO)], axis=0)
    col = col_in[1]
    for o in range(NO):
        cblk = new.at[o * KO : (o + 1) * KO]
        cs_out[o * 32 : (o + 1) * 32, :] = mm(owner_onehot(col, o), cblk[...]).astype(BF16)
        shift = jnp.concatenate([logv[o * 8 + q : o * 8 + q + 1, :] for q in range(8)], axis=1)
        score_block(x, cblk, gs[o], acc, shift, o == 0)
    finish_rows(acc, row_out)
    save.wait()


def last_potentials(rec, codes, tv):
    tot = rec[0, 0:16, :].astype(F32)
    for d in range(1, ND):
        tot = tot + rec[d, 0:16, :].astype(F32)
    tot = jnp.concatenate([tot[0:8], tot[8:16]], axis=1)
    some = codes[...] > 0.0
    return jnp.where(some, tv[...] / jnp.where(some, tot, 1.0), 0.0)


def tail_kernel(rec, codes, tv, col_in, xs_in, cs_in, w_in, mass1, out):
    vs = last_potentials(rec, codes, tv)
    mass2 = w_in[...] * column(own_row(vs))
    lane = iota((SL, 128), 1)
    m = jnp.where(lane == 0, mass1[...], jnp.where(lane == 1, mass2, 0.0))
    pos = (codes[...] - 1.0).astype(jnp.int32)
    col = col_in[1]
    new = []
    for o in range(NO):
        mine = col[o * 32 : (o + 1) * 32, :] - 1.0
        mine = jnp.concatenate([mine, mine], axis=1).astype(jnp.int32)
        oht = jnp.where(mine == pos[o : o + 1, :], vs[o : o + 1, :], 0.0).astype(BF16)
        z = cs_in[o * 32 : (o + 1) * 32, :].astype(F32) + mm(oht, slot_rows(o, rec, 16))
        new.append(unit(z).astype(BF16).astype(F32))
    r = xs_in[1].astype(F32) - jnp.concatenate(new, axis=0)
    both = jnp.concatenate([r.astype(BF16), m.astype(BF16)], axis=1)
    both = mm(order_matrix(True), both).astype(BF16)
    for s in range(NC):
        out[s, 0:16, :] = both[s * 16 : (s + 1) * 16, 0:128]
        out[s, 16:32, :] = both[s * 16 : (s + 1) * 16, 128:256]


def last_kernel(rec, codes, tv, old, new):
    vs = last_potentials(rec, codes, tv)
    pos = (codes[...] - 1.0).astype(jnp.int32)
    for o in range(NO):
        refine(o, pos[o : o + 1, :], vs[o : o + 1, :], slot_rows(o, rec, 16), old, new)


def exchange(x, axis):
    return lax.all_to_all(x, axis, 0, 0, tiled=True)


def on_device(embeddings, centroids, col_mass, assignments):
    target = col_mass.reshape(KC // 128, 128)
    gshape = tuple(pltpu.VMEM((T, KO), BF16) for _ in range(NO))
    sums = shape(NC, NC, 128, dtype=BF16)
    racc = (pltpu.VMEM((T, 128), F32),)
    pay = call(
        pack_kernel,
        shape(NC, TOK + 16, 128, dtype=BF16),
        "pack",
        10**6,
        8,
        (pltpu.VMEM((TOK, D), BF16), pltpu.VMEM((2, TOK), jnp.int32), pltpu.SemaphoreType.DMA((2,))),
        in_specs=[pl.BlockSpec(memory_space=pltpu.HBM)] * 2,
    )(*(pltpu.with_memory_space_constraint(a, pltpu.HBM) for a in (embeddings, assignments)))
    rec = exchange(pay, "cent")
    c0 = call(cent_kernel, shape(KC, D, dtype=BF16), "cents", 10**9, 12)(centroids)
    p, xs, ids, col, cs = call(
        slot_kernel,
        (
            shape(2, SL, TOK),
            shape(2, SL, D, dtype=BF16),
            shape(16, 128, dtype=BF16),
            shape(2, SL, 128),
            shape(SL, D, dtype=BF16),
        ),
        "slots",
        10**9,
        12,
    )(rec, c0)
    rec, c0, xs = lax.optimization_barrier((rec, c0, xs))

    def columns(it, rows, cs, meta, g):
        def body(*refs):
            colsum_kernel(it, *refs)

        out, w = call(
            body,
            (shape(ND, 272 if it else 336, 128, dtype=BF16), shape(SL, 128)),
            f"columns{it}",
            10**9,
            12,
            (pltpu.VMEM((T, 128), BF16), pltpu.VMEM((64, 128), F32)),
        )(rows, p, xs, cs, meta, *g)
        return exchange(out, "dp"), w

    *g, x, rows = call(
        first_kernel, gshape + (pltpu.VMEM((T, 2 * D), BF16), sums), "first", 10**10, 12, racc
    )(rec, c0)
    rows = exchange(rows, "cent")
    got, w = columns(0, rows, cs, ids, g)
    vmem = pl.BlockSpec(memory_space=pltpu.VMEM)
    *g, c1, rows, mass1, cs, codes, tv = call(
        second_kernel,
        gshape
        + (
            pltpu.HBM((KC, D), BF16),
            sums,
            shape(SL, 128),
            shape(SL, D, dtype=BF16),
            shape(NO, SL),
            shape(NO, SL),
        ),
        "second",
        10**10,
        12,
        racc + (pltpu.VMEM((KC // 128, 128), F32), pltpu.VMEM((KC, D), BF16), pltpu.SemaphoreType.DMA),
        out_specs=(vmem,) * NO + (pl.BlockSpec(memory_space=pltpu.HBM),) + (vmem,) * 5,
    )(got, target, col, w, c0, x)
    rows = exchange(rows, "cent")
    got, w = columns(1, rows, cs, codes, g)
    out = call(tail_kernel, shape(NC, 32, 128, dtype=BF16), "tail", 10**8, 12)(
        got, codes, tv, col, xs, cs, w, mass1
    )
    got, out = lax.optimization_barrier((got, out))
    back = exchange(out, "cent")
    c2 = call(last_kernel, shape(KC, D, dtype=BF16), "last", 10**9, 12)(got, codes, tv, c1)
    mass, res = call(unpack_kernel, (shape(2, TOK), shape(TOK, D, dtype=BF16)), "unpack", 10**6, 8)(
        assignments, back
    )
    return c2, mass, res


def solution(mesh):
    in_specs = (P(("dp", "cent"), None), P("cent", None), P("cent"), P(None, ("dp", "cent")))
    out_specs = (P("cent", None), P(None, ("dp", "cent")), P(("dp", "cent"), None))
    return jax.shard_map(
        on_device, mesh=mesh, in_specs=in_specs, out_specs=out_specs, check_vma=False
    )
```

```python
import math

import jax
import jax.numpy as jnp
from jax import lax
from jax.experimental import pallas as pl
from jax.experimental.pallas import tpu as pltpu
from jax.sharding import PartitionSpec as P

F32, BF16 = jnp.float32, jnp.bfloat16
D = 128
TOK = 128
NC, ND = 16, 8
T = TOK * NC
KC = 8192
NO, KO = 8, 1024
SL = 256
SCALE = 20.0 * math.log2(math.e)
TOKENS, CENTROIDS = 16384, 131072
TR = 256
MIB = 2**20

NN = (((1,), (0,)), ((), ()))
NT = (((1,), (1,)), ((), ()))


def mm(a, b, dims=NN):
    return lax.dot_general(a, b, dims, preferred_element_type=F32)


def iota(shape, dim):
    return lax.broadcasted_iota(jnp.int32, shape, dim)


def unit(z):
    return z * lax.rsqrt(jnp.sum(z * z, axis=1, keepdims=True) + 1e-06)


def split(z):
    hi = z.astype(BF16)
    return hi, (z - hi.astype(F32)).astype(BF16)


def column(row):
    return jnp.concatenate(
        [
            jnp.broadcast_to(row[:, i : i + 128], (128, 128)).T
            for i in range(0, row.shape[1], 128)
        ],
        axis=0,
    )


def call(body, outs, name, flops, limit, scratch=(), **specs):
    return pl.pallas_call(
        body,
        **specs,
        out_shape=outs,
        scratch_shapes=list(scratch),
        name=name,
        compiler_params=pltpu.CompilerParams(vmem_limit_bytes=limit * MIB),
        cost_estimate=pl.CostEstimate(
            flops=flops, bytes_accessed=2 * MIB, transcendentals=0
        ),
    )


def shape(*dims, dtype=F32):
    return jax.ShapeDtypeStruct(dims, dtype)


def pack_kernel(emb_hbm, asg_hbm, out, emb, asg, sems):
    copies = [
        pltpu.make_async_copy(emb_hbm, emb, sems.at[0]),
        pltpu.make_async_copy(asg_hbm, asg, sems.at[1]),
    ]
    for c in copies:
        c.start()
    for c in copies:
        c.wait()
    xn = unit(emb[...].astype(F32)).astype(BF16)
    rows = []
    for it in range(2):
        a = asg[it : it + 1, :]
        owner = a >> 10
        own_f = owner.astype(F32)
        same = jnp.broadcast_to(own_f, (TOK, TOK)).T == own_f
        before = iota((TOK, TOK), 0) < iota((TOK, TOK), 1)
        rank = jnp.sum(jnp.where(same & before, 1.0, 0.0), axis=0, keepdims=True)
        code = (a & (KO - 1)) + 1
        rows.append((a >> 13, code >> 5, code & 31, (owner & 7) * 2 + rank.astype(jnp.int32)))
    zero = jnp.zeros((5, TOK), jnp.int32)
    for c in range(NC):
        out[c, 0:TOK, :] = xn
        parts = []
        for shard, hi, lo, place in rows:
            mine = shard == c
            parts += [jnp.where(mine, hi, 0), jnp.where(mine, lo, 0), place, zero]
        out[c, TOK : TOK + 16, :] = jnp.concatenate(parts, axis=0).astype(F32).astype(BF16)


def place_kernel(asg, oh_out):
    for it in range(2):
        a = asg[it : it + 1, :]
        owner = a >> 10
        own_f = owner.astype(F32)
        same = jnp.broadcast_to(own_f, (TOK, TOK)).T == own_f
        before = iota((TOK, TOK), 0) < iota((TOK, TOK), 1)
        rank = jnp.sum(jnp.where(same & before, 1.0, 0.0), axis=0, keepdims=True)
        row = (a >> 13).astype(F32) * 16.0 + (owner & 7).astype(F32) * 2.0 + rank
        col = column(row)
        lane = iota((TOK, 128), 1).astype(F32)
        oh_out[it] = jnp.concatenate(
            [jnp.where(col == lane + 128.0 * j, 1.0, 0.0) for j in range(2)], axis=1
        ).astype(BF16)


def unpack_kernel(oh, rec, mass_out, res_out):
    mrows = jnp.concatenate([rec[s, 16:32, :] for s in range(NC)], axis=0)
    rrows = jnp.concatenate([rec[s, 0:16, :] for s in range(NC)], axis=0)
    res_out[...] = mm(oh[1], rrows).astype(BF16)
    pick = jnp.where(iota((8, 128), 0) == iota((8, 128), 1), 1.0, 0.0).astype(BF16)
    m = mm(pick, mrows, NT).astype(BF16)
    mass_out[0:1, :] = mm(m, oh[0], NT)[0:1, :]
    mass_out[1:2, :] = mm(m, oh[1], NT)[1:2, :]


def cent_kernel(cent, out):
    @pl.loop(0, KC // 256)
    def _(i):
        at = pl.ds(pl.multiple_of(i * 256, 256), 256)
        out[at, :] = unit(cent[at, :].astype(F32)).astype(BF16)


def score_rows(rec, x):
    for s in range(NC):
        hi, lo = split(rec[s, 0:TOK, :].astype(F32) * SCALE)
        x[s * TOK : (s + 1) * TOK, :] = jnp.concatenate([hi, lo], axis=1)


def score_block(x, cblk, g, acc, shift, first):
    c = jnp.concatenate([cblk[...], cblk[...]], axis=1)
    for r in range(0, T, TR):
        at = slice(r, r + TR)
        e = mm(x[at, :], c, NT)
        if shift is not None:
            e = e + shift
        e = jnp.exp2(e)
        g[at, :] = e.astype(BF16)
        part = e[:, 0:128]
        for q in range(128, KO, 128):
            part = part + e[:, q : q + 128]
        if first:
            acc[at, :] = part
        else:
            acc[at, :] += part


def finish_rows(acc, out):
    hi, lo = split(acc[...])
    one = jnp.ones((8, 128), BF16)
    r = mm(one, hi, NT) + mm(one, lo, NT)
    r = jnp.concatenate([r[0:1, s * 128 : (s + 1) * 128] for s in range(NC)], axis=0).astype(BF16)
    for c in range(NC):
        out[c] = r


def first_kernel(rec, cents, *refs):
    gs, (x, row_out, acc) = refs[:NO], refs[NO:]
    score_rows(rec, x)
    for o in range(NO):
        score_block(x, cents.at[o * KO : (o + 1) * KO], gs[o], acc, None, o == 0)
    finish_rows(acc, row_out)


def owner_onehot(idcol, o):
    ids = idcol[o * 32 : (o + 1) * 32, :]
    lane = iota((32, 128), 1).astype(F32)
    return jnp.concatenate(
        [jnp.where(ids == lane + (128.0 * j + 1.0), 1.0, 0.0) for j in range(KO // 128)],
        axis=1,
    ).astype(BF16)


def order_matrix(back):
    i, j = iota((SL, SL), 0), iota((SL, SL), 1)
    if back:
        want = ((i >> 1) & 7) * 32 + (i >> 4) * 2 + (i & 1)
    else:
        want = ((i >> 1) & 15) * 16 + (i >> 5) * 2 + (i & 1)
    return jnp.where(j == want, 1.0, 0.0).astype(BF16)


def slot_kernel(rec, cents, p_out, xs_out, id_out, col_out, cs_out):
    order = order_matrix(False)
    ids = []
    for it in range(2):
        base = TOK + 8 * it
        place16 = iota((16, TOK), 0).astype(F32)
        xs, digits = [], []
        for s in range(NC):
            meta = rec[s, base : base + 8, :].astype(F32)
            hi, lo, place = meta[0:1, :], meta[1:2, :], meta[2:3, :]
            p = jnp.where((place16 == place) & (hi + lo > 0.0), 1.0, 0.0)
            p_out[it, s * 16 : (s + 1) * 16, :] = p
            xs.append(mm(p.astype(BF16), rec[s, 0:TOK, :]))
            digits.append(
                jnp.concatenate(
                    [
                        jnp.broadcast_to(jnp.sum(p * q, axis=1, keepdims=True), (16, 128))
                        for q in (hi, lo)
                    ],
                    axis=1,
                )
            )
        both = jnp.concatenate([jnp.concatenate(xs, axis=0), jnp.concatenate(digits, axis=0)], axis=1)
        both = mm(order, both.astype(BF16))
        xs_out[it] = both[:, 0:128].astype(BF16)
        dhi, dlo = both[:, 128:256], both[:, 256:384]
        col = dhi * 32.0 + dlo
        col_out[it] = col
        rhi = jnp.concatenate([dhi[0:128].T[0:1], dhi[128:256].T[0:1]], axis=1)
        rlo = jnp.concatenate([dlo[0:128].T[0:1], dlo[128:256].T[0:1]], axis=1)
        at = (iota((SL, 128), 0) & 31) + 32 * it
        lane = jnp.where(iota((SL, 128), 1) == at, 1.0, 0.0).astype(BF16)
        own = iota((8, SL), 0) == (iota((8, SL), 1) >> 5)
        rows = jnp.concatenate([jnp.where(own, rhi, 0.0), jnp.where(own, rlo, 0.0)], axis=0)
        ids.append(mm(rows.astype(BF16), lane))
        if it == 0:
            for o in range(NO):
                cs_out[o * 32 : (o + 1) * 32, :] = mm(
                    owner_onehot(col, o), cents[o * KO : (o + 1) * KO, :]
                ).astype(BF16)
    id_out[...] = (ids[0] + ids[1]).astype(BF16)


def colsum_kernel(it, rowp, p_in, xs_in, cs_in, meta, *refs):
    gs, (out, w_out, ucol, tots) = refs[:NO], refs[NO:]
    u = 1.0 / jnp.sum(rowp[...].astype(F32), axis=0)
    for s in range(NC):
        ucol[s * 128 : (s + 1) * 128, :] = jnp.broadcast_to(u[s : s + 1, :], (128, 128)).T.astype(BF16)
    W = 512
    for o in range(NO):
        for h in range(KO // W):

            def body(j, acc):
                at = pl.ds(pl.multiple_of(j * 128, 128), 128)
                uu = ucol[at, :]
                prod = gs[o][at, h * W : (h + 1) * W] * jnp.concatenate([uu] * (W // 128), axis=1)
                prod = prod[0:64] + prod[64:128]
                prod = prod[0:32] + prod[32:64]
                prod = (prod[0:16] + prod[16:32]).astype(F32)
                return acc + (prod[0:8] + prod[8:16])

            acc = lax.fori_loop(0, T // 128, body, jnp.zeros((8, W), F32), unroll=8)
            tot = jnp.sum(acc, axis=0, keepdims=True)
            row = (o * KO + h * W) // 128
            for q in range(W // 128):
                tots[row + q : row + q + 1, :] = tot[:, q * 128 : (q + 1) * 128]
    us = jnp.concatenate(
        [
            jnp.sum(p_in[it, s * 16 : (s + 1) * 16, :] * u[s : s + 1, :], axis=1, keepdims=True)
            for s in range(NC)
        ],
        axis=0,
    )
    uhi, ulo = split(jnp.broadcast_to(us, (SL, 128)))
    both = mm(order_matrix(False), jnp.concatenate([uhi, ulo], axis=1))
    us = both[:, 0:128] + both[:, 128:256]
    xs = xs_in[it].astype(F32)
    aff = jnp.sum(xs * cs_in[...].astype(F32), axis=1, keepdims=True)
    w = (CENTROIDS * jnp.exp2(aff * SCALE)) * us
    w_out[...] = w
    rows = (w * xs).astype(BF16)
    if it == 0:
        tot = tots[...].astype(BF16)
    else:
        got = jnp.concatenate([slot_values(o, meta, tots)[1] for o in range(NO)], axis=0)
        tot = jnp.concatenate([got[:, 0:128], got[:, 128:256]], axis=0).astype(BF16)
    base = tot.shape[0]
    for d in range(ND):
        out[d, 0:base, :] = tot
        out[d, base : base + SL, :] = rows
        if it == 0:
            out[d, 320:336, :] = meta[...]


def slot_codes(rec, it):
    mine = (iota((16, 128), 1) >> 5) == it
    halves = []
    for h in range(2):
        tot = jnp.zeros((16, 128), F32)
        for q in range(4):
            ids = jnp.where(mine, rec[4 * h + q, 320:336, :].astype(F32), 0.0)
            by = 32 * ((q - it) % 4)
            tot = tot + (pltpu.roll(ids, by, 1) if by else ids)
        halves.append(tot)
    both = jnp.concatenate(halves, axis=1)
    return both[0:8] * 32.0 + both[8:16]


def own_row(values):
    at = lax.axis_index("dp") * 32 + (iota((SL, SL), 1) & 31)
    pick = jnp.where(iota((SL, SL), 0) == at, 1.0, 0.0).astype(BF16)
    hi, lo = split(values)
    got = mm(jnp.concatenate([hi, lo], axis=0), pick)
    got = got[0:8] + got[8:16]
    own = iota((8, SL), 0) == (iota((8, SL), 1) >> 5)
    return jnp.sum(jnp.where(own, got, 0.0), axis=0, keepdims=True)


def slot_values(o, codes, table):
    pos = (codes[o : o + 1, :] - 1.0).astype(jnp.int32)
    hi, lo = split(table[o * 8 : (o + 1) * 8, :])
    oh = jnp.where(iota((128, 256), 0) == (pos & 127), 1.0, 0.0).astype(BF16)
    got = mm(jnp.concatenate([hi, lo], axis=0), oh)
    got = got[0:8] + got[8:16]
    val = jnp.sum(jnp.where(iota((8, 256), 0) == (pos >> 7), got, 0.0), axis=0, keepdims=True)
    return pos, val


def slot_rows(o, rec, base):
    return jnp.concatenate(
        [rec[d, base + o * 32 : base + (o + 1) * 32, :] for d in range(ND)], axis=0
    )


def refine(o, pos, vs, rows, old, new):
    oht = jnp.where(iota((KO, 256), 0) == pos, vs, 0.0).astype(BF16)
    at = slice(o * KO, (o + 1) * KO)
    z = old[at, :].astype(F32) + mm(oht, rows)
    new[at, :] = unit(z).astype(BF16)


def second_kernel(rec, target, col_in, w_in, old, x, *refs):
    gs, (new_hbm, row_out, mass_out, cs_out, code_out, tv_out) = refs[:NO], refs[NO : 6 + NO]
    acc, vbuf, new, sem = refs[6 + NO :]
    tot = rec[0, 0:64, :].astype(F32)
    for d in range(1, ND):
        tot = tot + rec[d, 0:64, :].astype(F32)
    goal = target[...] * (TOKENS / CENTROIDS)
    v = goal / tot
    vbuf[...] = v
    logv = jnp.log2(v)
    codes = slot_codes(rec, 0)
    slots = [slot_values(o, codes, vbuf) for o in range(NO)]
    for o in range(NO):
        refine(o, *slots[o], slot_rows(o, rec, 64), old, new)
    save = pltpu.make_async_copy(new, new_hbm, sem)
    save.start()
    vs = jnp.concatenate([val for _, val in slots], axis=0)
    mass_out[...] = w_in[...] * column(own_row(vs))
    codes = slot_codes(rec, 1)
    code_out[...] = codes
    vbuf[...] = goal * v
    tv_out[...] = jnp.concatenate([slot_values(o, codes, vbuf)[1] for o in range(NO)], axis=0)
    col = col_in[1]
    for o in range(NO):
        cblk = new.at[o * KO : (o + 1) * KO]
        cs_out[o * 32 : (o + 1) * 32, :] = mm(owner_onehot(col, o), cblk[...]).astype(BF16)
        shift = jnp.concatenate([logv[o * 8 + q : o * 8 + q + 1, :] for q in range(8)], axis=1)
        score_block(x, cblk, gs[o], acc, shift, o == 0)
    finish_rows(acc, row_out)
    save.wait()


def last_potentials(rec, codes, tv):
    tot = rec[0, 0:16, :].astype(F32)
    for d in range(1, ND):
        tot = tot + rec[d, 0:16, :].astype(F32)
    tot = jnp.concatenate([tot[0:8], tot[8:16]], axis=1)
    some = codes[...] > 0.0
    return jnp.where(some, tv[...] / jnp.where(some, tot, 1.0), 0.0)


def tail_kernel(rec, codes, tv, col_in, xs_in, cs_in, w_in, mass1, out):
    vs = last_potentials(rec, codes, tv)
    mass2 = w_in[...] * column(own_row(vs))
    lane = iota((SL, 128), 1)
    m = jnp.where(lane == 0, mass1[...], jnp.where(lane == 1, mass2, 0.0))
    pos = (codes[...] - 1.0).astype(jnp.int32)
    col = col_in[1]
    new = []
    for o in range(NO):
        mine = col[o * 32 : (o + 1) * 32, :] - 1.0
        mine = jnp.concatenate([mine, mine], axis=1).astype(jnp.int32)
        oht = jnp.where(mine == pos[o : o + 1, :], vs[o : o + 1, :], 0.0).astype(BF16)
        z = cs_in[o * 32 : (o + 1) * 32, :].astype(F32) + mm(oht, slot_rows(o, rec, 16))
        new.append(unit(z).astype(BF16).astype(F32))
    r = xs_in[1].astype(F32) - jnp.concatenate(new, axis=0)
    both = jnp.concatenate([r.astype(BF16), m.astype(BF16)], axis=1)
    both = mm(order_matrix(True), both).astype(BF16)
    for s in range(NC):
        out[s, 0:16, :] = both[s * 16 : (s + 1) * 16, 0:128]
        out[s, 16:32, :] = both[s * 16 : (s + 1) * 16, 128:256]


def last_kernel(rec, codes, tv, old, new):
    vs = last_potentials(rec, codes, tv)
    pos = (codes[...] - 1.0).astype(jnp.int32)
    for o in range(NO):
        refine(o, pos[o : o + 1, :], vs[o : o + 1, :], slot_rows(o, rec, 16), old, new)


def exchange(x, axis):
    return lax.all_to_all(x, axis, 0, 0, tiled=True)


def on_device(embeddings, centroids, col_mass, assignments):
    target = col_mass.reshape(KC // 128, 128)
    gshape = tuple(pltpu.VMEM((T, KO), BF16) for _ in range(NO))
    sums = shape(NC, NC, 128, dtype=BF16)
    racc = (pltpu.VMEM((T, 128), F32),)
    pay = call(
        pack_kernel,
        shape(NC, TOK + 16, 128, dtype=BF16),
        "pack",
        10**6,
        8,
        (pltpu.VMEM((TOK, D), BF16), pltpu.VMEM((2, TOK), jnp.int32), pltpu.SemaphoreType.DMA((2,))),
        in_specs=[pl.BlockSpec(memory_space=pltpu.HBM)] * 2,
    )(*(pltpu.with_memory_space_constraint(a, pltpu.HBM) for a in (embeddings, assignments)))
    rec = exchange(pay, "cent")
    oh = call(place_kernel, shape(2, TOK, SL, dtype=BF16), "places", 10**6, 8)(assignments)
    c0 = call(cent_kernel, shape(KC, D, dtype=BF16), "cents", 10**9, 12)(centroids)
    p, xs, ids, col, cs = call(
        slot_kernel,
        (
            shape(2, SL, TOK),
            shape(2, SL, D, dtype=BF16),
            shape(16, 128, dtype=BF16),
            shape(2, SL, 128),
            shape(SL, D, dtype=BF16),
        ),
        "slots",
        10**9,
        12,
    )(rec, c0)
    rec, c0, xs = lax.optimization_barrier((rec, c0, xs))

    def columns(it, rows, cs, meta, g):
        def body(*refs):
            colsum_kernel(it, *refs)

        out, w = call(
            body,
            (shape(ND, 272 if it else 336, 128, dtype=BF16), shape(SL, 128)),
            f"columns{it}",
            10**9,
            12,
            (pltpu.VMEM((T, 128), BF16), pltpu.VMEM((64, 128), F32)),
        )(rows, p, xs, cs, meta, *g)
        return exchange(out, "dp"), w

    *g, x, rows = call(
        first_kernel, gshape + (pltpu.VMEM((T, 2 * D), BF16), sums), "first", 10**10, 12, racc
    )(rec, c0)
    rows = exchange(rows, "cent")
    got, w = columns(0, rows, cs, ids, g)
    vmem = pl.BlockSpec(memory_space=pltpu.VMEM)
    *g, c1, rows, mass1, cs, codes, tv = call(
        second_kernel,
        gshape
        + (
            pltpu.HBM((KC, D), BF16),
            sums,
            shape(SL, 128),
            shape(SL, D, dtype=BF16),
            shape(NO, SL),
            shape(NO, SL),
        ),
        "second",
        10**10,
        12,
        racc + (pltpu.VMEM((KC // 128, 128), F32), pltpu.VMEM((KC, D), BF16), pltpu.SemaphoreType.DMA),
        out_specs=(vmem,) * NO + (pl.BlockSpec(memory_space=pltpu.HBM),) + (vmem,) * 5,
    )(got, target, col, w, c0, x)
    rows = exchange(rows, "cent")
    got, w = columns(1, rows, cs, codes, g)
    out = call(tail_kernel, shape(NC, 32, 128, dtype=BF16), "tail", 10**8, 12)(
        got, codes, tv, col, xs, cs, w, mass1
    )
    got, out = lax.optimization_barrier((got, out))
    back = exchange(out, "cent")
    c2 = call(last_kernel, shape(KC, D, dtype=BF16), "last", 10**9, 12)(got, codes, tv, c1)
    mass, res = call(unpack_kernel, (shape(2, TOK), shape(TOK, D, dtype=BF16)), "unpack", 10**6, 8)(
        oh, back
    )
    return c2, mass, res


def solution(mesh):
    in_specs = (P(("dp", "cent"), None), P("cent", None), P("cent"), P(None, ("dp", "cent")))
    out_specs = (P("cent", None), P(None, ("dp", "cent")), P(("dp", "cent"), None))
    return jax.shard_map(
        on_device, mesh=mesh, in_specs=in_specs, out_specs=out_specs, check_vma=False
    )
```
